256 devices in a mesh: seq: 64 (over z, y_lo, x), head: 4 (over y_hi, core).
Axes of the slice: x: 4, y: 4 (y_hi: 2, y_lo: 2; y = y_hi * 2 + y_lo), z: 8, core: 2. Of those that a mesh axis runs over, the one named last changes fastest.
Arguments:
- features: bfloat16 [8192, 4096], P('seq', 'head'), may hold values from -6 to 6
- queries: bfloat16 [8192, 1536], P('seq', 'head'), may hold values from -200 to 200
- keys: bfloat16 [8192, 1536], P('seq', 'head'), may hold values from -6 to 6
- router: bfloat16 [192, 4096], P('head'), may hold values from -0.09375 to 0.09375
- value_experts: bfloat16 [24, 8, 2048, 128], P('head', None, 'seq'), may hold values from -0.09375 to 0.09375
- output_experts: bfloat16 [24, 8, 2048, 128], P('head', None, 'seq'), may hold values from -3 to 3
- expert_ids: int32 [64, 24, 2], P(None, 'head'), may hold values from 0 to 7, all different within a row
Outputs:
- mixed: bfloat16 [8192, 4096], P('seq', 'head')
The draws below stay inside these ranges and needn't reach their ends.
All inputs are finite; a program needn't handle non-finite values.
Results may differ from the reference program's by a relative error of at most 0.022.
Values may be sent and summed in bfloat16 or wider, within the bound.
No kernel may reach another device: no remote copies, remote signals or barrier semaphores. Data moves between devices by JAX's collectives and lax.ppermute only.
A program may use at most 128 MiB of HBM per device.

```python
import math
import jax
import jax.numpy as jnp
from jax import lax

D = 4096
HEADS = 24
HEAD_SIZE = 64
EXPERTS = 8
TOP = 2
BLK = 128
SEQ = 8192
BLOCKS = 64


def paired(key):
    base_q = 2.0 * jax.random.normal(jax.random.fold_in(key, 11), (SEQ, HEADS * HEAD_SIZE), jnp.float32)
    base_k = jax.random.normal(jax.random.fold_in(key, 23), (SEQ, HEADS * HEAD_SIZE), jnp.float32)
    base_q = jnp.clip(base_q, -12.0, 12.0)
    base_k = jnp.clip(base_k, -6.0, 6.0)
    return (base_q, base_k)


def draw_queries(key, part):
    return paired(key)[0].astype(jnp.bfloat16)


def draw_keys(key, part):
    return paired(key)[1].astype(jnp.bfloat16)


def block_scale(key, dims, shards, least, top_value):
    level = 1.0
    for dim, shards_of in shards:
        heights = jax.random.uniform(jax.random.fold_in(jax.random.fold_in(key, 6), dim), (shards_of,), jnp.float32, least / len(shards), top_value / len(shards))
        level = level * jnp.repeat(jnp.exp(heights), dims[dim] // shards_of).reshape((-1,) + (1,) * (len(dims) - 1 - dim))
    return level


def picks_of(stream_key, rows, count, top, lift):
    order = jax.random.permutation(jax.random.fold_in(stream_key, 1), count)
    favour = order
    for power in range(3):
        favour = favour * favour // count
    favour = favour * lift // count
    lots = jax.random.randint(jax.random.fold_in(stream_key, 2), (rows, count), 0, 4096) + favour
    holders = jax.random.permutation(jax.random.fold_in(stream_key, 3), rows)[jnp.arange(count) % rows]
    lots = jnp.where(jnp.arange(rows)[:, None] == holders[None, :], 1 << 14, lots)
    merit = lots * count + jnp.arange(count)
    return lax.top_k(merit.astype(jnp.int32), top)[1].astype(jnp.int32)


def gaussian(own_key, dims, deviation, bound, cuts=(), held_as=jnp.bfloat16):
    factor_of = block_scale(own_key, dims, cuts, -0.22, 0.18) if cuts else 1.0
    entries = jax.random.normal(own_key, dims, jnp.float32) * deviation * factor_of
    return jnp.minimum(jnp.maximum(entries, -bound), bound).astype(held_as)


def setup_inputs(seed: int = 0) -> dict:
    splits = jax.random.split(jax.random.key(seed), 8)
    features = gaussian(splits[0], (SEQ, D), 1.0, 6.0, ((0, 64), (1, 4)))
    queries = draw_queries(jax.random.fold_in(splits[7], 71), 0)
    keys = draw_keys(jax.random.fold_in(splits[7], 71), 0)
    router = gaussian(splits[3], (HEADS * EXPERTS, D), D ** -0.5, 0.09375, ((0, 4),))
    value_experts = gaussian(splits[4], (HEADS, EXPERTS, D // 2, 2 * HEAD_SIZE), D ** -0.5, 0.09375, ((0, 4), (2, 64)))
    output_experts = gaussian(splits[5], (HEADS, EXPERTS, D // 2, 2 * HEAD_SIZE), (HEAD_SIZE // 16) ** -0.5, 3.0, ((0, 4), (2, 64)))
    expert_ids = picks_of(splits[6], BLOCKS * HEADS, EXPERTS, TOP, 2048).reshape((BLOCKS, HEADS, TOP))
    return dict(features=features, queries=queries, keys=keys, router=router, value_experts=value_experts, output_experts=output_experts, expert_ids=expert_ids)


masked_score = -1e+30

def reference(features, queries, keys, router, value_experts, output_experts, expert_ids):
    seq_len = features.shape[0]
    value_table = value_experts.reshape(HEADS, EXPERTS, D, HEAD_SIZE)
    output_table = output_experts.reshape(HEADS, EXPERTS, D, HEAD_SIZE)
    logits = jnp.einsum('td,ed->te', features, router, preferred_element_type=jnp.float32).reshape(seq_len, HEADS, EXPERTS)
    token_ids = jnp.repeat(expert_ids, BLK, axis=0)
    gates = jax.nn.sigmoid(jnp.take_along_axis(logits, token_ids, axis=2)).astype(jnp.bfloat16)
    x_blocks = features.reshape(BLOCKS, BLK, D).astype(jnp.float32)
    position = jnp.arange(seq_len, dtype=jnp.int32)
    causal = position[None, :] <= position[:, None]
    score_scale = 1.0 / math.sqrt(HEAD_SIZE)

    def one_head(summed, head_index):
        chosen = expert_ids[:, head_index, :]
        gate_part = gates[:, head_index, :].astype(jnp.float32).reshape(BLOCKS, BLK, TOP)
        value_rows = jnp.take(value_table[head_index], chosen, axis=0).astype(jnp.float32)
        raw_values = jnp.einsum('btd,bjdk->bjtk', x_blocks, value_rows)
        values = jnp.einsum('btj,bjtk->btk', gate_part, raw_values).reshape(seq_len, HEAD_SIZE).astype(jnp.bfloat16)
        first_col = (head_index * HEAD_SIZE).astype(jnp.int32)
        query_part = lax.dynamic_slice_in_dim(queries, first_col, HEAD_SIZE, 1)
        key_part = lax.dynamic_slice_in_dim(keys, first_col, HEAD_SIZE, 1)
        scores = jnp.dot(query_part, key_part.T, preferred_element_type=jnp.float32) * score_scale
        scores = jnp.where(causal, scores, masked_score)
        top_score = lax.optimization_barrier(jnp.max(scores, axis=1, keepdims=True))
        weights = jnp.where(causal, jnp.exp(scores - top_score), 0.0)
        attended = jnp.dot(weights.astype(jnp.bfloat16), values, preferred_element_type=jnp.float32)
        attended = (attended / lax.optimization_barrier(jnp.sum(weights, axis=1, keepdims=True))).astype(jnp.bfloat16)
        out_rows = jnp.take(output_table[head_index], chosen, axis=0).astype(jnp.float32)
        products = jnp.einsum('btk,bjck->btjc', attended.reshape(BLOCKS, BLK, HEAD_SIZE).astype(jnp.float32), out_rows)
        contrib = jnp.einsum('btj,btjc->btc', gate_part, products).reshape(seq_len, D)
        return (summed + contrib, None)
    summed, ignored = lax.scan(one_head, jnp.zeros((seq_len, D), jnp.float32), jnp.arange(HEADS, dtype=jnp.int32))
    return summed.astype(jnp.bfloat16)
```

```python
import math

import jax
import jax.numpy as jnp
from jax import lax
from jax.experimental import pallas as pl
from jax.experimental.pallas import tpu as pltpu
from jax.sharding import Mesh, PartitionSpec as P

TOP = 2
BLK = 128
SLABS = 8
PLANE = 8
HALF = 64
LANES = 128
AXES = ("z", "yl", "x", "yh", "c")
SEQ_AXES = ("z", "yl", "x")
HEAD_AXES = ("yh", "c")
PLANE_AXES = ("yl", "x")
bf16 = jnp.bfloat16
f32 = jnp.float32
i32 = jnp.int32
masked_score = -1e30
VMEM_BYTES = 56 * 1024 * 1024

smem = pl.BlockSpec(memory_space=pltpu.SMEM)
vmem = pl.BlockSpec(memory_space=pltpu.VMEM)
params = pltpu.CompilerParams(vmem_limit_bytes=VMEM_BYTES)


def cost(flops, nbytes, trans=0):
    return pl.CostEstimate(flops=flops, bytes_accessed=nbytes, transcendentals=trans)


def iota(shape, dim):
    return lax.broadcasted_iota(i32, shape, dim)


def one_hot(mask):
    return jnp.where(mask, 1.0, 0.0).astype(bf16)


def nt_dot(a, b):
    return lax.dot_general(a, b, (((1,), (1,)), ((), ())), preferred_element_type=f32)


def dot(a, b):
    return jnp.dot(a, b, preferred_element_type=f32)


def message_kernel(ids, place, f0, f1, f2, f3, router, out):
    slots = router.shape[0] // 8 * TOP
    quarter = f0.shape[1]
    seq, group = place[0], place[1]
    row, col = iota((LANES, router.shape[0]), 0), iota((LANES, router.shape[0]), 1)
    target = jnp.full(row.shape, -1, i32)
    for k in range(slots):
        target = jnp.where(row == k, (k // TOP) * 8 + ids[seq * slots + k], target)
    chosen = one_hot(col == target)
    logits = jnp.zeros((BLK, LANES), f32)
    for rel, part in enumerate((f0, f1, f2, f3)):
        first = pl.multiple_of((group ^ rel) * quarter, quarter)
        rows = dot(chosen, router[:, pl.ds(first, quarter)]).astype(bf16)
        logits = logits + nt_dot(part[...], rows)
        for pi in range(PLANE):
            low = part[:, pi * HALF : (pi + 1) * HALF]
            high = part[:, quarter // 2 + pi * HALF : quarter // 2 + (pi + 1) * HALF]
            out[pi, :, rel * LANES : (rel + 1) * LANES] = jnp.concatenate([low, high], axis=1)
    gates = jax.nn.sigmoid(logits).astype(bf16)
    for pi in range(PLANE):
        out[pi, :, 4 * LANES :] = gates


def pair_kernel(scale, queries, keys, out):
    for i in range(PLANE):
        if i * HALF < queries.shape[1]:
            own = slice(i * HALF, (i + 1) * HALF)
            out[i] = jnp.concatenate([queries[:, own] * bf16(scale), keys[:, own]], axis=1)
        else:
            out[i] = jnp.zeros((BLK, LANES), bf16)


def key_kernel(pairs, out):
    for q in range(PLANE // 2):
        out[q] = jnp.concatenate([pairs[2 * q][:, HALF:], pairs[2 * q + 1][:, HALF:]], axis=1)


def value_kernel(ids, place, message, table, out):
    heads = table.shape[1]
    z, group = place[2], place[1]
    src, dst = iota((512, 512), 0), iota((512, 512), 1)
    within = src & 63
    source_z = ((src >> 7) ^ group) * 2 + ((src >> 6) & 1)
    split = one_hot(dst == (within & 1) * 256 + source_z * 32 + (within >> 1))
    left = iota((BLK, LANES), 1) < HALF

    def two_blocks(q, carry):
        done = []
        for bb in range(2):
            b = 2 * q + bb
            x = dot(message[b, :, 0:512], split).astype(bf16)
            x = jnp.concatenate([x[:, :256], x[:, 256:]], axis=0)
            gates = message[b, :, 512:].astype(f32)
            sums = []
            for h in range(heads):
                total = 0.0
                picked = [
                    table[:, h, ids[((z * PLANE + b) * heads + h) * TOP + j]].reshape(256, LANES)
                    for j in range(TOP)
                ]
                r = dot(x, jnp.concatenate(picked, axis=1))
                for j in range(TOP):
                    cols = slice(j * LANES, (j + 1) * LANES)
                    k = h * TOP + j
                    total = total + gates[:, k : k + 1] * jnp.where(left, r[:BLK, cols], r[BLK:, cols])
                sums.append(total + pltpu.roll(total, HALF, 1))
            done.append(sums)
        for h in range(heads):
            out[h, q] = jnp.where(left, done[0][h], done[1][h]).astype(bf16)
        for h in range(heads, PLANE):
            out[h, q] = jnp.zeros((BLK, LANES), bf16)
        return carry

    lax.fori_loop(0, PLANE // 2, two_blocks, 0)


def weight_kernel(place, pairs, k0, k1, k2, k3, k4, k5, k6, k7, probs, sums, scores, tops, totals):
    block, z = pl.program_id(0), place[2]
    left = iota((BLK, LANES), 1) < HALF
    zero = jnp.zeros((BLK, HALF), bf16)
    own = pairs[0][:, :HALF]
    q = jnp.concatenate(
        [jnp.concatenate([own, zero], axis=1), jnp.concatenate([zero, own], axis=1)], axis=0
    )
    tops[...] = jnp.full(tops.shape, masked_score, f32)
    totals[...] = jnp.zeros(totals.shape, f32)

    for s, keys in enumerate((k0, k1, k2, k3, k4, k5, k6, k7)):

        @pl.when(s <= z)
        def _():
            got = nt_dot(q, keys[...])
            if s == 0:
                row, col = iota(got.shape, 0), iota(got.shape, 1)
                key_pos = (2 * (col >> 7) + (row >> 7)) * BLK + (col & 127)
                got = jnp.where(key_pos <= block * BLK + (row & 127), got, masked_score)
            scores[s] = got
            best = tops[...]
            for part in range(4):
                cols = slice(part * LANES, (part + 1) * LANES)
                best = jnp.maximum(best, jnp.maximum(got[:BLK, cols], got[BLK:, cols]))
            tops[...] = best

    top = jnp.max(tops[...], axis=1, keepdims=True)

    for s in range(SLABS):

        @pl.when(s <= z)
        def _():
            total = totals[...]
            for bb in range(2):
                p = jnp.exp(scores[s, bb * BLK : (bb + 1) * BLK, :] - top)
                for part in range(4):
                    total = total + p[:, part * LANES : (part + 1) * LANES]
                probs[s, bb] = p.astype(bf16)
            totals[...] = total

    sums[...] = jnp.broadcast_to(jnp.sum(totals[...], axis=1, keepdims=True), (BLK, LANES))


def attend_kernel(place, probs, sums, v0, v1, v2, v3, v4, v5, v6, v7, out, acc):
    step, z = pl.program_id(0), place[2]

    @pl.when(step == 0)
    def _():
        acc[...] = jnp.zeros(acc.shape, f32)

    for s, values in enumerate((v0, v1, v2, v3, v4, v5, v6, v7)):

        @pl.when((step == s) & (s <= z))
        def _():
            for bb in range(2):
                acc[bb] += dot(probs[0, bb], values[...])

    @pl.when(step == SLABS - 1)
    def _():
        left = iota((BLK, LANES), 1) < HALF
        for q in range(PLANE // 2):
            pair = []
            for bb in range(2):
                rows = slice((2 * q + bb) * BLK, (2 * q + bb + 1) * BLK)
                o = jnp.where(left, acc[0, rows], acc[1, rows])
                pair.append((o + pltpu.roll(o, HALF, 1)) / sums[rows])
            packed = jnp.where(left, pair[0], pair[1]).astype(bf16)
            for pi in range(PLANE):
                out[pi, q] = packed


def mix_kernel(ids, place, attended, gates_in, table, near, far, lhs, rhs, natural):
    heads = table.shape[1]
    z, group = place[2], place[1]
    src, dst = iota((512, 512), 0), iota((512, 512), 1)
    order = one_hot(dst == ((src & 255) >> 5) * 64 + 2 * (src & 31) + (src >> 8))
    left = iota((BLK, LANES), 1) < HALF

    def two_blocks(q, carry):
        for bb in range(2):
            b = 2 * q + bb
            gates = gates_in[b].astype(f32)
            for h in range(heads):
                half = attended[h, q][:, bb * HALF : (bb + 1) * HALF]
                both = jnp.concatenate([half, half], axis=1).astype(f32)
                for j in range(TOP):
                    k = h * TOP + j
                    cols = slice(k * LANES, (k + 1) * LANES)
                    gated = both * gates[:, k : k + 1]
                    lhs[0:BLK, cols] = jnp.where(left, gated, 0.0).astype(bf16)
                    lhs[BLK:, cols] = jnp.where(left, 0.0, gated).astype(bf16)
                    rhs[:, cols] = table[
                        :, h, ids[((z * PLANE + b) * heads + h) * TOP + j]
                    ].reshape(256, LANES)
            r = nt_dot(lhs[...], rhs[...])
            flat = jnp.concatenate([r[:BLK], r[BLK:]], axis=1).astype(bf16)
            flat = dot(flat, order).astype(bf16)
            for g in range(4):
                natural[g] = flat[:, g * LANES : (g + 1) * LANES]
            near[0, b] = natural[group]
            far[0, b] = natural[group ^ 1]
            near[1, b] = natural[group ^ 2]
            far[1, b] = natural[group ^ 3]
        return carry

    lax.fori_loop(0, PLANE // 2, two_blocks, 0)


def place_kernel(pieces, out):
    width = out.shape[1] // 2
    for low in range(2):
        own = slice(low * HALF, (low + 1) * HALF)
        for m in range(PLANE // 2):
            out[:, low * width + m * LANES : low * width + (m + 1) * LANES] = jnp.concatenate(
                [pieces[2 * m][:, own], pieces[2 * m + 1][:, own]], axis=1
            )


def swap(x, axis):
    return lax.ppermute(x, axis, [(0, 1), (1, 0)])


def plane_exchange(x):
    return lax.all_to_all(x, PLANE_AXES, split_axis=0, concat_axis=0, tiled=True)


def later_slabs(x):
    return [x] + [
        lax.ppermute(x, "z", [(i, i + s) for i in range(SLABS - s)]) for s in range(1, SLABS)
    ]


def add(a, b):
    return (a.astype(f32) + b.astype(f32)).astype(bf16)


def body(features, queries, keys, router, value_experts, output_experts, expert_ids):
    z = lax.axis_index("z")
    group = lax.axis_index(HEAD_AXES)
    seq = lax.axis_index(SEQ_AXES)
    place = jnp.stack([seq, group, z]).astype(i32)
    ids = expert_ids.reshape(-1)
    heads = value_experts.shape[0]
    scale = 1.0 / math.sqrt(HALF)

    value_table = lax.all_gather(value_experts, "z", axis=0, tiled=False)
    pairs = pl.pallas_call(
        lambda *refs: pair_kernel(scale, *refs),
        out_shape=jax.ShapeDtypeStruct((PLANE, BLK, LANES), bf16),
        in_specs=[vmem, vmem],
        out_specs=vmem,
        cost_estimate=cost(0, 500_000),
    )(queries, keys)
    pairs = plane_exchange(pairs)

    over_y = swap(features, "yh")
    over_c = swap(features, "c")
    over_yc = swap(over_y, "c")
    message = pl.pallas_call(
        message_kernel,
        out_shape=jax.ShapeDtypeStruct((PLANE, BLK, 5 * LANES), bf16),
        in_specs=[smem, smem] + [vmem] * 5,
        out_specs=vmem,
        compiler_params=params,
        cost_estimate=cost(2 * BLK * LANES * 4096 * 2, 3_000_000),
    )(ids, place, features, over_c, over_y, over_yc, router)
    message = plane_exchange(message)

    own_keys = pl.pallas_call(
        key_kernel,
        out_shape=jax.ShapeDtypeStruct((PLANE // 2, BLK, LANES), bf16),
        in_specs=[vmem],
        out_specs=vmem,
        cost_estimate=cost(0, 400_000),
    )(pairs).reshape(PLANE // 2 * BLK, LANES)
    key_parts = later_slabs(own_keys)

    slab = PLANE * BLK
    probs, sums = pl.pallas_call(
        weight_kernel,
        grid=(PLANE,),
        out_shape=(
            jax.ShapeDtypeStruct((SLABS, 2, slab, slab // 2), bf16),
            jax.ShapeDtypeStruct((slab, LANES), f32),
        ),
        in_specs=[smem, pl.BlockSpec((1, BLK, LANES), lambda i: (i, 0, 0))] + [vmem] * SLABS,
        out_specs=(
            pl.BlockSpec((SLABS, 2, BLK, slab // 2), lambda i: (0, 0, i, 0)),
            pl.BlockSpec((BLK, LANES), lambda i: (i, 0)),
        ),
        scratch_shapes=[
            pltpu.VMEM((SLABS, 2 * BLK, slab // 2), f32),
            pltpu.VMEM((BLK, LANES), f32),
            pltpu.VMEM((BLK, LANES), f32),
        ],
        compiler_params=params,
        cost_estimate=cost(2 * slab * SLABS * slab * 128, 18_000_000, slab * slab * SLABS),
    )(place, pairs, *key_parts)

    partial = pl.pallas_call(
        value_kernel,
        out_shape=jax.ShapeDtypeStruct((PLANE, PLANE // 2, BLK, LANES), bf16),
        in_specs=[smem, smem, vmem, vmem],
        out_specs=vmem,
        compiler_params=params,
        cost_estimate=cost(2 * 48 * 256 * 256 * 256, 6_000_000),
    )(ids, place, message, value_table)
    partial = plane_exchange(partial)
    own_values = jnp.sum(partial.astype(f32), axis=0).astype(bf16).reshape(slab // 2, LANES)
    value_parts = later_slabs(own_values)
    output_table = lax.all_gather(output_experts, "z", axis=0, tiled=False)

    attended = pl.pallas_call(
        attend_kernel,
        grid_spec=pltpu.PrefetchScalarGridSpec(
            num_scalar_prefetch=1,
            grid=(SLABS,),
            in_specs=[
                pl.BlockSpec((1, 2, slab, slab // 2), lambda s, at: (jnp.minimum(s, at[2]), 0, 0, 0)),
                pl.BlockSpec((slab, LANES), lambda s, at: (0, 0)),
            ]
            + [pl.BlockSpec((slab // 2, LANES), lambda s, at: (0, 0))] * SLABS,
            out_specs=pl.BlockSpec((PLANE, PLANE // 2, BLK, LANES), lambda s, at: (0, 0, 0, 0)),
            scratch_shapes=[pltpu.VMEM((2, slab, LANES), f32)],
        ),
        out_shape=jax.ShapeDtypeStruct((PLANE, PLANE // 2, BLK, LANES), bf16),
        compiler_params=params,
        cost_estimate=cost(2 * slab * SLABS * slab * 128, 18_000_000),
    )(place, probs, sums, *value_parts)
    attended = plane_exchange(attended)

    half_out = jax.ShapeDtypeStruct((2, PLANE, BLK, LANES), bf16)
    near, far = pl.pallas_call(
        mix_kernel,
        out_shape=(half_out, half_out),
        in_specs=[smem, smem, vmem, vmem, vmem],
        out_specs=(vmem, vmem),
        scratch_shapes=[
            pltpu.VMEM((2 * BLK, heads * TOP * LANES), bf16),
            pltpu.VMEM((256, heads * TOP * LANES), bf16),
            pltpu.VMEM((4, BLK, LANES), bf16),
        ],
        compiler_params=params,
        cost_estimate=cost(2 * 48 * 256 * 256 * 256, 6_000_000),
    )(ids, place, attended, message[:, :, 4 * LANES :], output_table)
    near = add(near, swap(far, "c"))
    mixed = add(near[0], swap(near[1], "yh"))
    mixed = plane_exchange(mixed)
    return pl.pallas_call(
        place_kernel,
        out_shape=jax.ShapeDtypeStruct(features.shape, bf16),
        in_specs=[vmem],
        out_specs=vmem,
        cost_estimate=cost(0, 600_000),
    )(mixed)


def solution(mesh):
    fine = Mesh(mesh.devices.reshape(SLABS, 2, 4, 2, 2), AXES)
    return jax.shard_map(
        body,
        mesh=fine,
        in_specs=(
            P(SEQ_AXES, HEAD_AXES),
            P(SEQ_AXES, HEAD_AXES),
            P(SEQ_AXES, HEAD_AXES),
            P(HEAD_AXES, None),
            P(HEAD_AXES, None, SEQ_AXES, None),
            P(HEAD_AXES, None, SEQ_AXES, None),
            P(None, HEAD_AXES, None),
        ),
        out_specs=P(SEQ_AXES, HEAD_AXES),
        check_vma=False,
    )
```

```python
import math

import jax
import jax.numpy as jnp
from jax import lax
from jax.experimental import pallas as pl
from jax.experimental.pallas import tpu as pltpu
from jax.sharding import Mesh, PartitionSpec as P

TOP = 2
BLK = 128
SLABS = 8
PLANE = 8
HALF = 64
LANES = 128
AXES = ("z", "yl", "x", "yh", "c")
SEQ_AXES = ("z", "yl", "x")
HEAD_AXES = ("yh", "c")
PLANE_AXES = ("yl", "x")
bf16 = jnp.bfloat16
f32 = jnp.float32
i32 = jnp.int32
masked_score = -1e30
VMEM_BYTES = 56 * 1024 * 1024

smem = pl.BlockSpec(memory_space=pltpu.SMEM)
vmem = pl.BlockSpec(memory_space=pltpu.VMEM)
params = pltpu.CompilerParams(vmem_limit_bytes=VMEM_BYTES)


def cost(flops, nbytes, trans=0):
    return pl.CostEstimate(flops=flops, bytes_accessed=nbytes, transcendentals=trans)


def iota(shape, dim):
    return lax.broadcasted_iota(i32, shape, dim)


def one_hot(mask):
    return jnp.where(mask, 1.0, 0.0).astype(bf16)


def nt_dot(a, b):
    return lax.dot_general(a, b, (((1,), (1,)), ((), ())), preferred_element_type=f32)


def dot(a, b):
    return jnp.dot(a, b, preferred_element_type=f32)


def message_kernel(ids, place, f0, f1, f2, f3, router, out):
    slots = router.shape[0] // 8 * TOP
    quarter = f0.shape[1]
    seq, group = place[0], place[1]
    row, col = iota((LANES, router.shape[0]), 0), iota((LANES, router.shape[0]), 1)
    target = jnp.full(row.shape, -1, i32)
    for k in range(slots):
        target = jnp.where(row == k, (k // TOP) * 8 + ids[seq * slots + k], target)
    chosen = one_hot(col == target)
    logits = jnp.zeros((BLK, LANES), f32)
    for rel, part in enumerate((f0, f1, f2, f3)):
        first = pl.multiple_of((group ^ rel) * quarter, quarter)
        rows = dot(chosen, router[:, pl.ds(first, quarter)]).astype(bf16)
        logits = logits + nt_dot(part[...], rows)
        for pi in range(PLANE):
            low = part[:, pi * HALF : (pi + 1) * HALF]
            high = part[:, quarter // 2 + pi * HALF : quarter // 2 + (pi + 1) * HALF]
            out[pi, :, rel * LANES : (rel + 1) * LANES] = jnp.concatenate([low, high], axis=1)
    gates = jax.nn.sigmoid(logits).astype(bf16)
    for pi in range(PLANE):
        out[pi, :, 4 * LANES :] = gates


def pair_kernel(scale, queries, keys, out):
    for i in range(PLANE):
        if i * HALF < queries.shape[1]:
            own = slice(i * HALF, (i + 1) * HALF)
            out[i] = jnp.concatenate([queries[:, own] * bf16(scale), keys[:, own]], axis=1)
        else:
            out[i] = jnp.zeros((BLK, LANES), bf16)


def key_kernel(pairs, out):
    for q in range(PLANE // 2):
        both = jnp.concatenate([pairs[2 * q][:, HALF:], pairs[2 * q + 1][:, HALF:]], axis=1)
        out[:, q * BLK : (q + 1) * BLK] = both.T


def value_kernel(ids, place, message, table, out):
    heads = table.shape[1]
    z, group = place[2], place[1]
    src, dst = iota((512, 512), 0), iota((512, 512), 1)
    within = src & 63
    source_z = ((src >> 7) ^ group) * 2 + ((src >> 6) & 1)
    split = one_hot(dst == (within & 1) * 256 + source_z * 32 + (within >> 1))
    left = iota((BLK, LANES), 1) < HALF

    def two_blocks(q, carry):
        done = []
        for bb in range(2):
            b = 2 * q + bb
            x = dot(message[b, :, 0:512], split).astype(bf16)
            x = jnp.concatenate([x[:, :256], x[:, 256:]], axis=0)
            gates = message[b, :, 512:].astype(f32)
            sums = []
            for h in range(heads):
                total = 0.0
                picked = [
                    table[:, h, ids[((z * PLANE + b) * heads + h) * TOP + j]].reshape(256, LANES)
                    for j in range(TOP)
                ]
                r = dot(x, jnp.concatenate(picked, axis=1))
                for j in range(TOP):
                    cols = slice(j * LANES, (j + 1) * LANES)
                    k = h * TOP + j
                    total = total + gates[:, k : k + 1] * jnp.where(left, r[:BLK, cols], r[BLK:, cols])
                sums.append(total + pltpu.roll(total, HALF, 1))
            done.append(sums)
        for h in range(heads):
            out[h, q] = jnp.where(left, done[0][h], done[1][h]).astype(bf16)
        for h in range(heads, PLANE):
            out[h, q] = jnp.zeros((BLK, LANES), bf16)
        return carry

    lax.fori_loop(0, PLANE // 2, two_blocks, 0)


def weight_kernel(place, pairs, k0, k1, k2, k3, k4, k5, k6, k7, probs, sums, even, odd, even_top, odd_top, totals):
    step, z = pl.program_id(0), place[2]
    block = jnp.minimum(step, PLANE - 1)
    zero = jnp.zeros((BLK, HALF), bf16)
    own = pairs[0][:, :HALF]
    q = jnp.concatenate(
        [jnp.concatenate([own, zero], axis=1), jnp.concatenate([zero, own], axis=1)], axis=0
    )

    def run(scores, tops, old_scores, old_tops):
        top = jnp.broadcast_to(jnp.max(old_tops[...], axis=1, keepdims=True), (BLK, LANES))
        tops[...] = jnp.full((BLK, LANES), masked_score, f32)
        totals[...] = jnp.zeros(totals.shape, f32)
        for s, keys in enumerate((k0, k1, k2, k3, k4, k5, k6, k7)):

            @pl.when(s <= z)
            def _():
                for c in range(2):
                    wide = slice(c * 256, (c + 1) * 256)
                    got = dot(q, keys[:, wide])
                    if s == 0:
                        row, col = iota(got.shape, 0), iota(got.shape, 1) + c * 256
                        key_pos = (2 * (col >> 7) + (row >> 7)) * BLK + (col & 127)
                        got = jnp.where(key_pos <= block * BLK + (row & 127), got, masked_score)
                    scores[s, :, wide] = got
                    tops[...] = jnp.maximum(
                        tops[...],
                        jnp.maximum(
                            jnp.maximum(got[:BLK, :LANES], got[:BLK, LANES:]),
                            jnp.maximum(got[BLK:, :LANES], got[BLK:, LANES:]),
                        ),
                    )
                    total = totals[...]
                    for bb in range(2):
                        for part in range(2 * c, 2 * c + 2):
                            cols = slice(part * LANES, (part + 1) * LANES)
                            p = jnp.exp(old_scores[s, bb * BLK : (bb + 1) * BLK, cols] - top)
                            total = total + p
                            probs[s, bb, :, cols] = p.astype(bf16)
                    totals[...] = total

        sums[...] = jnp.broadcast_to(jnp.sum(totals[...], axis=1, keepdims=True), (BLK, LANES))

    @pl.when(step % 2 == 0)
    def _():
        run(even, even_top, odd, odd_top)

    @pl.when(step % 2 == 1)
    def _():
        run(odd, odd_top, even, even_top)


def attend_kernel(near, carried, last, place, probs, *refs):
    values, refs = refs[: len(near)], refs[len(near) :]
    acc_in, out, acc = refs[:carried], refs[carried], refs[carried + 1]
    step, z = pl.program_id(0), place[2]
    left = iota((PLANE * BLK, LANES), 1) < HALF

    @pl.when(step == 0)
    def _():
        acc[...] = acc_in[0][...] if carried else jnp.zeros(acc.shape, f32)

    for k, s in enumerate(near):

        @pl.when((step == k) & (s <= z))
        def _():
            got = [dot(probs[0, bb], values[k][...]) for bb in range(2)]
            acc[...] += jnp.where(left, got[0], got[1])

    @pl.when(step == len(near) - 1)
    def _():
        if not last:
            out[...] = acc[...]
        else:
            left = iota((BLK, LANES), 1) < HALF
            for q in range(PLANE // 2):
                pair = []
                for bb in range(2):
                    rows = slice((2 * q + bb) * BLK, (2 * q + bb + 1) * BLK)
                    o = acc[rows]
                    pair.append((o + pltpu.roll(o, HALF, 1)) / acc_in[1][rows])
                packed = jnp.where(left, pair[0], pair[1]).astype(bf16)
                for pi in range(PLANE):
                    out[pi, q] = packed


def mix_kernel(ids, place, attended, gates_in, table, near, far, lhs, rhs, natural):
    heads = table.shape[1]
    z, group = place[2], place[1]
    src, dst = iota((512, 512), 0), iota((512, 512), 1)
    order = one_hot(dst == ((src & 255) >> 5) * 64 + 2 * (src & 31) + (src >> 8))
    left = iota((BLK, LANES), 1) < HALF

    def two_blocks(q, carry):
        for bb in range(2):
            b = 2 * q + bb
            gates = gates_in[b].astype(f32)
            for h in range(heads):
                half = attended[h, q][:, bb * HALF : (bb + 1) * HALF]
                both = jnp.concatenate([half, half], axis=1).astype(f32)
                for j in range(TOP):
                    k = h * TOP + j
                    cols = slice(k * LANES, (k + 1) * LANES)
                    gated = both * gates[:, k : k + 1]
                    lhs[0:BLK, cols] = jnp.where(left, gated, 0.0).astype(bf16)
                    lhs[BLK:, cols] = jnp.where(left, 0.0, gated).astype(bf16)
                    rhs[:, cols] = table[
                        :, h, ids[((z * PLANE + b) * heads + h) * TOP + j]
                    ].reshape(256, LANES)
            r = nt_dot(lhs[...], rhs[...])
            flat = jnp.concatenate([r[:BLK], r[BLK:]], axis=1).astype(bf16)
            flat = dot(flat, order).astype(bf16)
            for g in range(4):
                natural[g] = flat[:, g * LANES : (g + 1) * LANES]
            core = group & 1
            for y in range(2):
                near[y, b] = natural[2 * y + core]
                far[y, b] = natural[2 * y + (1 - core)]
        return carry

    lax.fori_loop(0, PLANE // 2, two_blocks, 0)


def place_kernel(pieces, out):
    width = out.shape[1] // 2
    summed = [(pieces[i].astype(f32) + pieces[PLANE + i].astype(f32)).astype(bf16) for i in range(PLANE)]
    for low in range(2):
        own = slice(low * HALF, (low + 1) * HALF)
        for m in range(PLANE // 2):
            out[:, low * width + m * LANES : low * width + (m + 1) * LANES] = jnp.concatenate(
                [summed[2 * m][:, own], summed[2 * m + 1][:, own]], axis=1
            )


def swap(x, axis):
    return lax.ppermute(x, axis, [(0, 1), (1, 0)])


def plane_exchange(x):
    return lax.all_to_all(x, PLANE_AXES, split_axis=0, concat_axis=0, tiled=True)


def ring(x):
    up = [(i, (i + 1) % SLABS) for i in range(SLABS)]
    down = [(i, (i - 1) % SLABS) for i in range(SLABS)]
    parts = [x] * SLABS
    for k in range(1, SLABS // 2):
        parts[k] = lax.ppermute(parts[k - 1], "z", up)
        parts[SLABS - k] = lax.ppermute(parts[(SLABS - k + 1) % SLABS], "z", down)
    parts[SLABS // 2] = lax.ppermute(parts[SLABS // 2 - 1], "z", up)
    return parts


def add(a, b):
    return (a.astype(f32) + b.astype(f32)).astype(bf16)


def body(features, queries, keys, router, value_experts, output_experts, expert_ids):
    z = lax.axis_index("z")
    group = lax.axis_index(HEAD_AXES)
    seq = lax.axis_index(SEQ_AXES)
    place = jnp.stack([seq, group, z]).astype(i32)
    ids = expert_ids.reshape(-1)
    heads = value_experts.shape[0]
    scale = 1.0 / math.sqrt(HALF)

    value_table = lax.all_gather(value_experts, "z", axis=0, tiled=False)
    pairs = pl.pallas_call(
        lambda *refs: pair_kernel(scale, *refs),
        out_shape=jax.ShapeDtypeStruct((PLANE, BLK, LANES), bf16),
        in_specs=[vmem, vmem],
        out_specs=vmem,
        cost_estimate=cost(0, 500_000),
    )(queries, keys)
    features, sent = lax.optimization_barrier((features, pairs))
    pairs = plane_exchange(sent)

    over_y = swap(features, "yh")
    over_c = swap(features, "c")
    over_yc = swap(over_y, "c")
    over_yc, pairs = lax.optimization_barrier((over_yc, pairs))
    message = pl.pallas_call(
        message_kernel,
        out_shape=jax.ShapeDtypeStruct((PLANE, BLK, 5 * LANES), bf16),
        in_specs=[smem, smem] + [vmem] * 5,
        out_specs=vmem,
        compiler_params=params,
        cost_estimate=cost(2 * BLK * LANES * 4096 * 2, 3_000_000),
    )(ids, place, features, over_c, over_y, over_yc, router)
    message = plane_exchange(message)

    own_keys = pl.pallas_call(
        key_kernel,
        out_shape=jax.ShapeDtypeStruct((LANES, PLANE // 2 * BLK), bf16),
        in_specs=[vmem],
        out_specs=vmem,
        cost_estimate=cost(0, 400_000),
    )(pairs)
    key_parts = ring(own_keys)
    message, key_parts = lax.optimization_barrier((message, key_parts))

    slab = PLANE * BLK
    partial = pl.pallas_call(
        value_kernel,
        out_shape=jax.ShapeDtypeStruct((PLANE, PLANE // 2, BLK, LANES), bf16),
        in_specs=[smem, smem, vmem, vmem],
        out_specs=vmem,
        compiler_params=params,
        cost_estimate=cost(2 * 48 * 256 * 256 * 256, 6_000_000),
    )(ids, place, message, value_table)
    _, pairs = lax.optimization_barrier((partial, pairs))
    probs, sums = pl.pallas_call(
        weight_kernel,
        grid=(PLANE + 1,),
        out_shape=(
            jax.ShapeDtypeStruct((SLABS, 2, slab, slab // 2), bf16),
            jax.ShapeDtypeStruct((slab, LANES), f32),
        ),
        in_specs=[smem, pl.BlockSpec((1, BLK, LANES), lambda i: (jnp.minimum(i, PLANE - 1), 0, 0))] + [vmem] * SLABS,
        out_specs=(
            pl.BlockSpec((SLABS, 2, BLK, slab // 2), lambda i: (0, 0, jnp.maximum(i - 1, 0), 0)),
            pl.BlockSpec((BLK, LANES), lambda i: (jnp.maximum(i - 1, 0), 0)),
        ),
        scratch_shapes=[
            pltpu.VMEM((SLABS, 2 * BLK, slab // 2), f32),
            pltpu.VMEM((SLABS, 2 * BLK, slab // 2), f32),
            pltpu.VMEM((BLK, LANES), f32),
            pltpu.VMEM((BLK, LANES), f32),
            pltpu.VMEM((BLK, LANES), f32),
        ],
        compiler_params=params,
        cost_estimate=cost(2 * slab * SLABS * slab * 128, 18_000_000, slab * slab * SLABS),
    )(place, pairs, *key_parts)

    partial = plane_exchange(partial)
    own_values = jnp.sum(partial.astype(f32), axis=0).astype(bf16).reshape(slab // 2, LANES)
    own_values, sums = lax.optimization_barrier((own_values, sums))
    values = ring(own_values)
    output_table = lax.all_gather(output_experts, "z", axis=0, tiled=False)

    def weighted(near, carried, last):
        steps = len(near)
        full = pl.BlockSpec((slab, LANES), lambda i, at: (0, 0))
        one = pl.BlockSpec((slab // 2, LANES), lambda i, at: (0, 0))

        def pick(i, at):
            s = jnp.int32(near[-1])
            for k in range(steps - 1):
                s = jnp.where(i == k, near[k], s)
            return (jnp.where(s <= at[2], s, 0), 0, 0, 0)

        if last:
            out_shape = jax.ShapeDtypeStruct((PLANE, PLANE // 2, BLK, LANES), bf16)
            out_spec = pl.BlockSpec(out_shape.shape, lambda i, at: (0, 0, 0, 0))
        else:
            out_shape = jax.ShapeDtypeStruct((slab, LANES), f32)
            out_spec = full
        return pl.pallas_call(
            lambda *refs: attend_kernel(near, len(carried), last, *refs),
            grid_spec=pltpu.PrefetchScalarGridSpec(
                num_scalar_prefetch=1,
                grid=(steps,),
                in_specs=[pl.BlockSpec((1, 2, slab, slab // 2), pick)]
                + [one] * steps
                + [full] * len(carried),
                out_specs=out_spec,
                scratch_shapes=[pltpu.VMEM((slab, LANES), f32)],
            ),
            out_shape=out_shape,
            compiler_params=params,
            cost_estimate=cost(steps * 2 * slab * slab * 128, steps * 2_000_000),
        )(place, probs, *[values[s] for s in near], *carried)

    acc = weighted((0, 1, 7), (), False)
    acc = weighted((2, 6, 3, 5), (acc,), False)
    attended = weighted((4,), (acc, sums), True)
    attended = plane_exchange(attended)

    half_out = jax.ShapeDtypeStruct((2, PLANE, BLK, LANES), bf16)
    near, far = pl.pallas_call(
        mix_kernel,
        out_shape=(half_out, half_out),
        in_specs=[smem, smem, vmem, vmem, vmem],
        out_specs=(vmem, vmem),
        scratch_shapes=[
            pltpu.VMEM((2 * BLK, heads * TOP * LANES), bf16),
            pltpu.VMEM((256, heads * TOP * LANES), bf16),
            pltpu.VMEM((4, BLK, LANES), bf16),
        ],
        compiler_params=params,
        cost_estimate=cost(2 * 48 * 256 * 256 * 256, 6_000_000),
    )(ids, place, attended, message[:, :, 4 * LANES :], output_table)
    near = add(near, swap(far, "c"))
    mixed = lax.all_to_all(
        near.reshape(2 * PLANE, BLK, LANES), ("yh",) + PLANE_AXES, split_axis=0, concat_axis=0, tiled=True
    )
    return pl.pallas_call(
        place_kernel,
        out_shape=jax.ShapeDtypeStruct(features.shape, bf16),
        in_specs=[vmem],
        out_specs=vmem,
        cost_estimate=cost(0, 600_000),
    )(mixed)


def solution(mesh):
    fine = Mesh(mesh.devices.reshape(SLABS, 2, 4, 2, 2), AXES)
    return jax.shard_map(
        body,
        mesh=fine,
        in_specs=(
            P(SEQ_AXES, HEAD_AXES),
            P(SEQ_AXES, HEAD_AXES),
            P(SEQ_AXES, HEAD_AXES),
            P(HEAD_AXES, None),
            P(HEAD_AXES, None, SEQ_AXES, None),
            P(HEAD_AXES, None, SEQ_AXES, None),
            P(None, HEAD_AXES, None),
        ),
        out_specs=P(SEQ_AXES, HEAD_AXES),
        check_vma=False,
    )
```

```python
import math

import jax
import jax.numpy as jnp
from jax import lax
from jax.experimental import pallas as pl
from jax.experimental.pallas import tpu as pltpu
from jax.sharding import Mesh, PartitionSpec as P

TOP = 2
BLK = 128
SLABS = 8
PLANE = 8
HALF = 64
LANES = 128
AXES = ("z", "yl", "x", "yh", "c")
SEQ_AXES = ("z", "yl", "x")
HEAD_AXES = ("yh", "c")
PLANE_AXES = ("yl", "x")
bf16 = jnp.bfloat16
f32 = jnp.float32
i32 = jnp.int32
masked_score = -1e30
VMEM_BYTES = 56 * 1024 * 1024

smem = pl.BlockSpec(memory_space=pltpu.SMEM)
vmem = pl.BlockSpec(memory_space=pltpu.VMEM)
params = pltpu.CompilerParams(vmem_limit_bytes=VMEM_BYTES)


def cost(flops, nbytes, trans=0):
    return pl.CostEstimate(flops=flops, bytes_accessed=nbytes, transcendentals=trans)


def iota(shape, dim):
    return lax.broadcasted_iota(i32, shape, dim)


def one_hot(mask):
    return jnp.where(mask, 1.0, 0.0).astype(bf16)


def nt_dot(a, b):
    return lax.dot_general(a, b, (((1,), (1,)), ((), ())), preferred_element_type=f32)


def dot(a, b):
    return jnp.dot(a, b, preferred_element_type=f32)


def message_kernel(ids, place, f0, f1, f2, f3, router, out):
    slots = router.shape[0] // 8 * TOP
    quarter = f0.shape[1]
    seq, group = place[0], place[1]
    row, col = iota((LANES, router.shape[0]), 0), iota((LANES, router.shape[0]), 1)
    target = jnp.full(row.shape, -1, i32)
    for k in range(slots):
        target = jnp.where(row == k, (k // TOP) * 8 + ids[seq * slots + k], target)
    chosen = one_hot(col == target)
    logits = jnp.zeros((BLK, LANES), f32)
    for rel, part in enumerate((f0, f1, f2, f3)):
        first = pl.multiple_of((group ^ rel) * quarter, quarter)
        rows = dot(chosen, router[:, pl.ds(first, quarter)]).astype(bf16)
        logits = logits + nt_dot(part[...], rows)
        for pi in range(PLANE):
            low = part[:, pi * HALF : (pi + 1) * HALF]
            high = part[:, quarter // 2 + pi * HALF : quarter // 2 + (pi + 1) * HALF]
            out[pi, :, rel * LANES : (rel + 1) * LANES] = jnp.concatenate([low, high], axis=1)
    gates = jax.nn.sigmoid(logits).astype(bf16)
    for pi in range(PLANE):
        out[pi, :, 4 * LANES :] = gates


def pair_kernel(scale, queries, keys, out):
    for i in range(PLANE):
        if i * HALF < queries.shape[1]:
            own = slice(i * HALF, (i + 1) * HALF)
            out[i] = jnp.concatenate([queries[:, own] * bf16(scale), keys[:, own]], axis=1)
        else:
            out[i] = jnp.zeros((BLK, LANES), bf16)


def key_kernel(pairs, out):
    for q in range(PLANE // 2):
        both = jnp.concatenate([pairs[2 * q][:, HALF:], pairs[2 * q + 1][:, HALF:]], axis=1)
        out[:, q * BLK : (q + 1) * BLK] = both.T


def value_kernel(ids, place, message, table, out):
    heads = table.shape[1]
    z, group = place[2], place[1]
    src, dst = iota((512, 512), 0), iota((512, 512), 1)
    within = src & 63
    source_z = ((src >> 7) ^ group) * 2 + ((src >> 6) & 1)
    split = one_hot(dst == (within & 1) * 256 + source_z * 32 + (within >> 1))
    left = iota((BLK, LANES), 1) < HALF

    def two_blocks(q, carry):
        done = []
        for bb in range(2):
            b = 2 * q + bb
            x = dot(message[b, :, 0:512], split).astype(bf16)
            x = jnp.concatenate([x[:, :256], x[:, 256:]], axis=0)
            gates = message[b, :, 512:].astype(f32)
            sums = []
            for h in range(heads):
                total = 0.0
                picked = [
                    table[:, h, ids[((z * PLANE + b) * heads + h) * TOP + j]].reshape(256, LANES)
                    for j in range(TOP)
                ]
                r = dot(x, jnp.concatenate(picked, axis=1))
                for j in range(TOP):
                    cols = slice(j * LANES, (j + 1) * LANES)
                    k = h * TOP + j
                    total = total + gates[:, k : k + 1] * jnp.where(left, r[:BLK, cols], r[BLK:, cols])
                sums.append(total)
            done.append(sums)
        for h in range(heads):
            first, second = done[0][h], done[1][h]
            crossed = pltpu.roll(jnp.where(left, second, first), HALF, 1)
            out[h, q] = (jnp.where(left, first, second) + crossed).astype(bf16)
        for h in range(heads, PLANE):
            out[h, q] = jnp.zeros((BLK, LANES), bf16)
        return carry

    lax.fori_loop(0, PLANE // 2, two_blocks, 0)


def weight_kernel(place, pairs, k0, k1, k2, k3, k4, k5, k6, k7, probs, sums, even, odd, even_top, odd_top, totals):
    step, z = pl.program_id(0), place[2]
    block = jnp.minimum(step, PLANE - 1)
    zero = jnp.zeros((BLK, HALF), bf16)
    own = pairs[0][:, :HALF]
    q = jnp.concatenate(
        [jnp.concatenate([own, zero], axis=1), jnp.concatenate([zero, own], axis=1)], axis=0
    )

    def run(scores, tops, old_scores, old_tops):
        top = jnp.broadcast_to(jnp.max(old_tops[...], axis=1, keepdims=True), (BLK, LANES))
        tops[...] = jnp.full((BLK, LANES), masked_score, f32)
        totals[...] = jnp.zeros(totals.shape, f32)
        every = (k0, k1, k2, k3, k4, k5, k6, k7)
        for first in range(0, SLABS, 2):

            @pl.when(first <= z)
            def _():
                best, total = tops[...], totals[...]
                for s in (first, first + 1):
                    for c in range(2):
                        wide = slice(c * 256, (c + 1) * 256)
                        got = dot(q, every[s][:, wide])
                        if s == 0:
                            row, col = iota(got.shape, 0), iota(got.shape, 1) + c * 256
                            key_pos = (2 * (col >> 7) + (row >> 7)) * BLK + (col & 127)
                            got = jnp.where(key_pos <= block * BLK + (row & 127), got, masked_score)
                        if s % 2 == 1:
                            got = jnp.where(s <= z, got, masked_score)
                        scores[s, :, wide] = got
                        for rows in (slice(0, BLK), slice(BLK, 2 * BLK)):
                            for cols in (slice(0, LANES), slice(LANES, 2 * LANES)):
                                best = jnp.maximum(best, got[rows, cols])
                        for bb in range(2):
                            for part in range(2 * c, 2 * c + 2):
                                cols = slice(part * LANES, (part + 1) * LANES)
                                p = jnp.exp(old_scores[s, bb * BLK : (bb + 1) * BLK, cols] - top)
                                total = total + p
                                probs[s, bb, :, cols] = p.astype(bf16)
                tops[...], totals[...] = best, total

        sums[...] = jnp.broadcast_to(jnp.sum(totals[...], axis=1, keepdims=True), (BLK, LANES))

    @pl.when(step % 2 == 0)
    def _():
        run(even, even_top, odd, odd_top)

    @pl.when(step % 2 == 1)
    def _():
        run(odd, odd_top, even, even_top)


def attend_kernel(near, carried, last, place, probs, *refs):
    values, refs = refs[: len(near)], refs[len(near) :]
    acc_in, out, acc = refs[:carried], refs[carried], refs[carried + 1]
    step, z = pl.program_id(0), place[2]
    left = iota((PLANE * BLK, LANES), 1) < HALF

    @pl.when(step == 0)
    def _():
        acc[...] = acc_in[0][...] if carried else jnp.zeros(acc.shape, f32)

    for k, s in enumerate(near):

        @pl.when((step == k) & (s <= z))
        def _():
            got = [dot(probs[0, bb], values[k][...]) for bb in range(2)]
            acc[...] += jnp.where(left, got[0], got[1])

    @pl.when(step == len(near) - 1)
    def _():
        if not last:
            out[...] = acc[...]
        else:
            left = iota((BLK, LANES), 1) < HALF
            for q in range(PLANE // 2):
                pair = []
                for bb in range(2):
                    rows = slice((2 * q + bb) * BLK, (2 * q + bb + 1) * BLK)
                    o = acc[rows]
                    pair.append((o + pltpu.roll(o, HALF, 1)) / acc_in[1][rows])
                packed = jnp.where(left, pair[0], pair[1]).astype(bf16)
                for pi in range(PLANE):
                    out[pi, q] = packed


def chosen_kernel(ids, place, table, out, flipped, ordered):
    b, z = pl.program_id(0), place[2]
    heads, experts = table.shape[1], table.shape[2]

    @pl.when(b == 0)
    def _():
        src, dst = iota((512, 512), 0), iota((512, 512), 1)
        order = one_hot(dst == ((src & 255) >> 5) * 64 + 2 * (src & 31) + (src >> 8))

        def one_head(h, carry):
            for e in range(experts):
                t = table[:, h, e].reshape(256, LANES).T
                first = pl.multiple_of(h * experts * HALF, experts * HALF) + e * HALF
                flipped[pl.ds(first, HALF), :] = jnp.concatenate([t[:HALF], t[HALF:]], axis=1)
            whole = pl.ds(pl.multiple_of(h * experts * HALF, experts * HALF), experts * HALF)
            ordered[whole, :] = dot(flipped[whole, :], order).astype(bf16)
            return carry

        lax.fori_loop(0, heads, one_head, 0)

    for k in range(heads * TOP):
        e = ids[(z * PLANE + b) * heads * TOP + k]
        first = pl.multiple_of(((k // TOP) * experts + e) * HALF, HALF)
        out[0, k * HALF : (k + 1) * HALF, :] = ordered[pl.ds(first, HALF), :]


def mix_kernel(place, attended, gates_in, rows, near, far, lhs, natural, spread):
    q, core = pl.program_id(0), place[1] & 1
    heads = rows.shape[1] // LANES
    left = iota((BLK, LANES), 1) < HALF

    @pl.when(q == 0)
    def _():
        spread[...] = one_hot(iota(spread.shape, 0) == (iota(spread.shape, 1) >> 6))

    for bb in range(2):
        gates = dot(gates_in[bb], spread[...])
        for h in range(heads):
            packed = attended[h, q].astype(f32)
            both = jnp.where(left == (bb == 0), packed, pltpu.roll(packed, HALF, 1))
            cols = slice(h * LANES, (h + 1) * LANES)
            lhs[bb, :, cols] = (both * gates[:, cols]).astype(bf16)
    for bb in range(2):
        flat = dot(lhs[bb], rows[bb]).astype(bf16)
        for g in range(4):
            natural[g, bb] = flat[:, g * LANES : (g + 1) * LANES]
    for y in range(2):
        near[y] = natural[2 * y + core]
        far[y] = natural[2 * y + (1 - core)]


def place_kernel(pieces, out):
    width = out.shape[1] // 2
    summed = [(pieces[i].astype(f32) + pieces[PLANE + i].astype(f32)).astype(bf16) for i in range(PLANE)]
    for low in range(2):
        own = slice(low * HALF, (low + 1) * HALF)
        for m in range(PLANE // 2):
            out[:, low * width + m * LANES : low * width + (m + 1) * LANES] = jnp.concatenate(
                [summed[2 * m][:, own], summed[2 * m + 1][:, own]], axis=1
            )


def swap(x, axis):
    return lax.ppermute(x, axis, [(0, 1), (1, 0)])


def plane_exchange(x):
    return lax.all_to_all(x, PLANE_AXES, split_axis=0, concat_axis=0, tiled=True)


def ring_step(x, way):
    return lax.ppermute(x, "z", [(i, (i + way) % SLABS) for i in range(SLABS)])


def add(a, b):
    return (a.astype(f32) + b.astype(f32)).astype(bf16)


def body(features, queries, keys, router, value_experts, output_experts, expert_ids):
    z = lax.axis_index("z")
    group = lax.axis_index(HEAD_AXES)
    seq = lax.axis_index(SEQ_AXES)
    place = jnp.stack([seq, group, z]).astype(i32)
    ids = expert_ids.reshape(-1)
    heads = value_experts.shape[0]
    scale = 1.0 / math.sqrt(HALF)

    value_table = lax.all_gather(value_experts, "z", axis=0, tiled=False)
    pairs = pl.pallas_call(
        lambda *refs: pair_kernel(scale, *refs),
        out_shape=jax.ShapeDtypeStruct((PLANE, BLK, LANES), bf16),
        in_specs=[vmem, vmem],
        out_specs=vmem,
        cost_estimate=cost(0, 500_000),
    )(queries, keys)
    pairs = plane_exchange(pairs)

    own_keys = pl.pallas_call(
        key_kernel,
        out_shape=jax.ShapeDtypeStruct((LANES, PLANE // 2 * BLK), bf16),
        in_specs=[vmem],
        out_specs=vmem,
        cost_estimate=cost(0, 400_000),
    )(pairs)
    keys = [own_keys] * SLABS
    keys[1], keys[7] = ring_step(own_keys, 1), ring_step(own_keys, -1)
    over_y = swap(features, "yh")
    over_c = swap(features, "c")
    over_yc = swap(over_y, "c")
    keys[2], keys[6] = ring_step(keys[1], 1), ring_step(keys[7], -1)
    message = pl.pallas_call(
        message_kernel,
        out_shape=jax.ShapeDtypeStruct((PLANE, BLK, 5 * LANES), bf16),
        in_specs=[smem, smem] + [vmem] * 5,
        out_specs=vmem,
        compiler_params=params,
        cost_estimate=cost(2 * BLK * LANES * 4096 * 2, 3_000_000),
    )(ids, place, features, over_c, over_y, over_yc, router)
    keys[3], keys[5] = ring_step(keys[2], 1), ring_step(keys[6], -1)
    message = plane_exchange(message)

    keys[4] = ring_step(keys[3], 1)
    message, keys = lax.optimization_barrier((message, keys))

    slab = PLANE * BLK
    partial = pl.pallas_call(
        value_kernel,
        out_shape=jax.ShapeDtypeStruct((PLANE, PLANE // 2, BLK, LANES), bf16),
        in_specs=[smem, smem, vmem, vmem],
        out_specs=vmem,
        compiler_params=params,
        cost_estimate=cost(2 * 48 * 256 * 256 * 256, 6_000_000),
    )(ids, place, message, value_table)
    _, pairs = lax.optimization_barrier((partial, pairs))
    probs, sums = pl.pallas_call(
        weight_kernel,
        grid=(PLANE + 1,),
        out_shape=(
            jax.ShapeDtypeStruct((SLABS, 2, slab, slab // 2), bf16),
            jax.ShapeDtypeStruct((slab, LANES), f32),
        ),
        in_specs=[smem, pl.BlockSpec((1, BLK, LANES), lambda i: (jnp.minimum(i, PLANE - 1), 0, 0))] + [vmem] * SLABS,
        out_specs=(
            pl.BlockSpec((SLABS, 2, BLK, slab // 2), lambda i: (0, 0, jnp.maximum(i - 1, 0), 0)),
            pl.BlockSpec((BLK, LANES), lambda i: (jnp.maximum(i - 1, 0), 0)),
        ),
        scratch_shapes=[
            pltpu.VMEM((SLABS, 2 * BLK, slab // 2), f32),
            pltpu.VMEM((SLABS, 2 * BLK, slab // 2), f32),
            pltpu.VMEM((BLK, LANES), f32),
            pltpu.VMEM((BLK, LANES), f32),
            pltpu.VMEM((BLK, LANES), f32),
        ],
        compiler_params=params,
        cost_estimate=cost(2 * slab * SLABS * slab * 128, 18_000_000, slab * slab * SLABS),
    )(place, pairs, *keys)

    partial = plane_exchange(partial)
    own_values = jnp.sum(partial.astype(f32), axis=0).astype(bf16).reshape(slab // 2, LANES)
    own_values, sums = lax.optimization_barrier((own_values, sums))
    values = [own_values] * SLABS
    output_table = lax.all_gather(output_experts, "z", axis=0, tiled=False)

    def weighted(near, carried, last):
        steps = len(near)
        full = pl.BlockSpec((slab, LANES), lambda i, at: (0, 0))
        one = pl.BlockSpec((slab // 2, LANES), lambda i, at: (0, 0))

        def pick(i, at):
            s = jnp.int32(near[-1])
            for k in range(steps - 1):
                s = jnp.where(i == k, near[k], s)
            return (jnp.where(s <= at[2], s, 0), 0, 0, 0)

        if last:
            out_shape = jax.ShapeDtypeStruct((PLANE, PLANE // 2, BLK, LANES), bf16)
            out_spec = pl.BlockSpec(out_shape.shape, lambda i, at: (0, 0, 0, 0))
        else:
            out_shape = jax.ShapeDtypeStruct((slab, LANES), f32)
            out_spec = full
        return pl.pallas_call(
            lambda *refs: attend_kernel(near, len(carried), last, *refs),
            grid_spec=pltpu.PrefetchScalarGridSpec(
                num_scalar_prefetch=1,
                grid=(steps,),
                in_specs=[pl.BlockSpec((1, 2, slab, slab // 2), pick)]
                + [one] * steps
                + [full] * len(carried),
                out_specs=out_spec,
                scratch_shapes=[pltpu.VMEM((slab, LANES), f32)],
            ),
            out_shape=out_shape,
            compiler_params=params,
            cost_estimate=cost(steps * 2 * slab * slab * 128, steps * 2_000_000),
        )(place, probs, *[values[s] for s in near], *carried)

    values[1], values[7] = ring_step(own_values, 1), ring_step(own_values, -1)
    acc = weighted((0,), (), False)
    values[1], values[7], acc = lax.optimization_barrier((values[1], values[7], acc))
    values[2], values[6] = ring_step(values[1], 1), ring_step(values[7], -1)
    acc = weighted((1, 7), (acc,), False)
    values[2], values[6], acc = lax.optimization_barrier((values[2], values[6], acc))
    values[3], values[5] = ring_step(values[2], 1), ring_step(values[6], -1)
    acc = weighted((2, 6), (acc,), False)
    values[3], values[5], acc = lax.optimization_barrier((values[3], values[5], acc))
    values[4] = ring_step(values[3], 1)
    acc = weighted((3, 5), (acc,), False)
    attended = weighted((4,), (acc, sums), True)
    _, output_table = lax.optimization_barrier((attended, output_table))
    attended = plane_exchange(attended)

    width = heads * TOP * HALF
    rows = pl.pallas_call(
        chosen_kernel,
        grid=(PLANE,),
        out_shape=jax.ShapeDtypeStruct((PLANE, width, 512), bf16),
        in_specs=[smem, smem, vmem],
        out_specs=pl.BlockSpec((1, width, 512), lambda b: (b, 0, 0)),
        scratch_shapes=[pltpu.VMEM((heads * 8 * HALF, 512), bf16)] * 2,
        compiler_params=params,
        cost_estimate=cost(0, 20_000_000),
    )(ids, place, output_table)
    half_out = jax.ShapeDtypeStruct((2, PLANE, BLK, LANES), bf16)
    half_spec = pl.BlockSpec((2, 2, BLK, LANES), lambda b: (0, b, 0, 0))
    near, far = pl.pallas_call(
        mix_kernel,
        grid=(PLANE // 2,),
        out_shape=(half_out, half_out),
        in_specs=[
            smem,
            vmem,
            pl.BlockSpec((2, BLK, LANES), lambda b: (b, 0, 4)),
            pl.BlockSpec((2, width, 512), lambda b: (b, 0, 0)),
        ],
        out_specs=(half_spec, half_spec),
        scratch_shapes=[
            pltpu.VMEM((2, BLK, width), bf16),
            pltpu.VMEM((4, 2, BLK, LANES), bf16),
            pltpu.VMEM((LANES, width), bf16),
        ],
        compiler_params=params,
        cost_estimate=cost(2 * 8 * 128 * 768 * 512, 8_000_000),
    )(place, attended, message, rows)
    near = add(near, swap(far, "c"))
    mixed = lax.all_to_all(
        near.reshape(2 * PLANE, BLK, LANES), ("yh",) + PLANE_AXES, split_axis=0, concat_axis=0, tiled=True
    )
    return pl.pallas_call(
        place_kernel,
        out_shape=jax.ShapeDtypeStruct(features.shape, bf16),
        in_specs=[vmem],
        out_specs=vmem,
        cost_estimate=cost(0, 600_000),
    )(mixed)


def solution(mesh):
    fine = Mesh(mesh.devices.reshape(SLABS, 2, 4, 2, 2), AXES)
    return jax.shard_map(
        body,
        mesh=fine,
        in_specs=(
            P(SEQ_AXES, HEAD_AXES),
            P(SEQ_AXES, HEAD_AXES),
            P(SEQ_AXES, HEAD_AXES),
            P(HEAD_AXES, None),
            P(HEAD_AXES, None, SEQ_AXES, None),
            P(HEAD_AXES, None, SEQ_AXES, None),
            P(None, HEAD_AXES, None),
        ),
        out_specs=P(SEQ_AXES, HEAD_AXES),
        check_vma=False,
    )
```

```python
import math

import jax
import jax.numpy as jnp
from jax import lax
from jax.experimental import pallas as pl
from jax.experimental.pallas import tpu as pltpu
from jax.sharding import Mesh, PartitionSpec as P

TOP = 2
BLK = 128
SLABS = 8
PLANE = 8
HALF = 64
LANES = 128
AXES = ("z", "yl", "x", "yh", "c")
SEQ_AXES = ("z", "yl", "x")
HEAD_AXES = ("yh", "c")
PLANE_AXES = ("yl", "x")
bf16 = jnp.bfloat16
f32 = jnp.float32
i32 = jnp.int32
masked_score = -1e30
MIB = 1024 * 1024

smem = pl.BlockSpec(memory_space=pltpu.SMEM)
vmem = pl.BlockSpec(memory_space=pltpu.VMEM)
large = pltpu.CompilerParams(vmem_limit_bytes=56 * MIB)
small = pltpu.CompilerParams(vmem_limit_bytes=20 * MIB)


def cost(flops, nbytes, trans=0):
    return pl.CostEstimate(flops=flops, bytes_accessed=nbytes, transcendentals=trans)


def iota(shape, dim):
    return lax.broadcasted_iota(i32, shape, dim)


def one_hot(mask):
    return jnp.where(mask, 1.0, 0.0).astype(bf16)


def nt_dot(a, b):
    return lax.dot_general(a, b, (((1,), (1,)), ((), ())), preferred_element_type=f32)


def dot(a, b):
    return jnp.dot(a, b, preferred_element_type=f32)


def message_kernel(ids, place, f0, f1, f2, f3, router, out):
    slots = router.shape[0] // 8 * TOP
    quarter = f0.shape[1]
    seq, group = place[0], place[1]
    row, col = iota((LANES, router.shape[0]), 0), iota((LANES, router.shape[0]), 1)
    target = jnp.full(row.shape, -1, i32)
    for k in range(slots):
        target = jnp.where(row == k, (k // TOP) * 8 + ids[seq * slots + k], target)
    chosen = one_hot(col == target)
    logits = jnp.zeros((BLK, LANES), f32)
    for rel, part in enumerate((f0, f1, f2, f3)):
        first = pl.multiple_of((group ^ rel) * quarter, quarter)
        rows = dot(chosen, router[:, pl.ds(first, quarter)]).astype(bf16)
        logits = logits + nt_dot(part[...], rows)
        for pi in range(PLANE):
            low = part[:, pi * HALF : (pi + 1) * HALF]
            high = part[:, quarter // 2 + pi * HALF : quarter // 2 + (pi + 1) * HALF]
            out[pi, :, rel * LANES : (rel + 1) * LANES] = jnp.concatenate([low, high], axis=1)
    gates = jax.nn.sigmoid(logits).astype(bf16)
    for pi in range(PLANE):
        out[pi, :, 4 * LANES :] = gates


def pair_kernel(scale, queries, keys, out):
    for i in range(PLANE):
        if i * HALF < queries.shape[1]:
            own = slice(i * HALF, (i + 1) * HALF)
            out[i] = jnp.concatenate([queries[:, own] * bf16(scale), keys[:, own]], axis=1)
        else:
            out[i] = jnp.zeros((BLK, LANES), bf16)


def key_kernel(pairs, out):
    for q in range(PLANE // 2):
        both = jnp.concatenate([pairs[2 * q][:, HALF:], pairs[2 * q + 1][:, HALF:]], axis=1)
        out[:, q * BLK : (q + 1) * BLK] = both.T


def value_kernel(ids, place, message, table, out):
    heads = table.shape[1]
    z, group = place[2], place[1]
    src, dst = iota((512, 512), 0), iota((512, 512), 1)
    within = src & 63
    source_z = ((src >> 7) ^ group) * 2 + ((src >> 6) & 1)
    split = one_hot(dst == (within & 1) * 256 + source_z * 32 + (within >> 1))
    left = iota((BLK, LANES), 1) < HALF

    def two_blocks(q, carry):
        done = []
        for bb in range(2):
            b = 2 * q + bb
            x = dot(message[b, :, 0:512], split).astype(bf16)
            x = jnp.concatenate([x[:, :256], x[:, 256:]], axis=0)
            gates = message[b, :, 512:].astype(f32)
            sums = []
            for h in range(heads):
                total = 0.0
                picked = [
                    table[:, h, ids[((z * PLANE + b) * heads + h) * TOP + j]].reshape(256, LANES)
                    for j in range(TOP)
                ]
                r = dot(x, jnp.concatenate(picked, axis=1))
                for j in range(TOP):
                    cols = slice(j * LANES, (j + 1) * LANES)
                    k = h * TOP + j
                    total = total + gates[:, k : k + 1] * jnp.where(left, r[:BLK, cols], r[BLK:, cols])
                sums.append(total)
            done.append(sums)
        for h in range(heads):
            first, second = done[0][h], done[1][h]
            crossed = pltpu.roll(jnp.where(left, second, first), HALF, 1)
            out[h, q] = (jnp.where(left, first, second) + crossed).astype(bf16)
        for h in range(heads, PLANE):
            out[h, q] = jnp.zeros((BLK, LANES), bf16)
        return carry

    lax.fori_loop(0, PLANE // 2, two_blocks, 0)


def weight_kernel(place, pairs, k0, k1, k2, k3, k4, k5, k6, k7, probs, sums, even, odd, even_top, odd_top, totals):
    step, z = pl.program_id(0), place[2]
    block = jnp.minimum(step, PLANE - 1)
    zero = jnp.zeros((BLK, HALF), bf16)
    own = pairs[0][:, :HALF]
    q = jnp.concatenate(
        [jnp.concatenate([own, zero], axis=1), jnp.concatenate([zero, own], axis=1)], axis=0
    )

    def run(scores, tops, old_scores, old_tops):
        top = jnp.broadcast_to(jnp.max(old_tops[...], axis=1, keepdims=True), (BLK, LANES))
        tops[...] = jnp.full((BLK, LANES), masked_score, f32)
        totals[...] = jnp.zeros(totals.shape, f32)
        every = (k0, k1, k2, k3, k4, k5, k6, k7)
        for first in range(0, SLABS, 2):

            @pl.when(first <= z)
            def _():
                best, total = tops[...], totals[...]
                for s in (first, first + 1):
                    for c in range(2):
                        wide = slice(c * 256, (c + 1) * 256)
                        got = dot(q, every[s][:, wide])
                        if s == 0:
                            row, col = iota(got.shape, 0), iota(got.shape, 1) + c * 256
                            key_pos = (2 * (col >> 7) + (row >> 7)) * BLK + (col & 127)
                            got = jnp.where(key_pos <= block * BLK + (row & 127), got, masked_score)
                        if s % 2 == 1:
                            got = jnp.where(s <= z, got, masked_score)
                        scores[s, :, wide] = got
                        for rows in (slice(0, BLK), slice(BLK, 2 * BLK)):
                            for cols in (slice(0, LANES), slice(LANES, 2 * LANES)):
                                best = jnp.maximum(best, got[rows, cols])
                        for bb in range(2):
                            for part in range(2 * c, 2 * c + 2):
                                cols = slice(part * LANES, (part + 1) * LANES)
                                p = jnp.exp(old_scores[s, bb * BLK : (bb + 1) * BLK, cols] - top)
                                total = total + p
                                probs[s, bb, :, cols] = p.astype(bf16)
                tops[...], totals[...] = best, total

        sums[...] = jnp.broadcast_to(jnp.sum(totals[...], axis=1, keepdims=True), (BLK, LANES))

    @pl.when(step % 2 == 0)
    def _():
        run(even, even_top, odd, odd_top)

    @pl.when(step % 2 == 1)
    def _():
        run(odd, odd_top, even, even_top)


def attend_kernel(near, carried, last, place, probs, *refs):
    values, refs = refs[: len(near)], refs[len(near) :]
    acc_in, out, acc = refs[:carried], refs[carried], refs[carried + 1]
    step, z = pl.program_id(0), place[2]
    left = iota((PLANE * BLK, LANES), 1) < HALF

    @pl.when(step == 0)
    def _():
        acc[...] = acc_in[0][...] if carried else jnp.zeros(acc.shape, f32)

    for k, s in enumerate(near):

        @pl.when((step == k) & (s <= z))
        def _():
            got = [dot(probs[0, bb], values[k][...]) for bb in range(2)]
            acc[...] += jnp.where(left, got[0], got[1])

    @pl.when(step == len(near) - 1)
    def _():
        if not last:
            out[...] = acc[...]
        else:
            left = iota((BLK, LANES), 1) < HALF
            for q in range(PLANE // 2):
                pair = []
                for bb in range(2):
                    rows = slice((2 * q + bb) * BLK, (2 * q + bb + 1) * BLK)
                    o = acc[rows]
                    pair.append((o + pltpu.roll(o, HALF, 1)) / acc_in[1][rows])
                packed = jnp.where(left, pair[0], pair[1]).astype(bf16)
                for pi in range(PLANE):
                    out[pi, q] = packed


def chosen_kernel(ids, place, table, out, flipped, ordered):
    b, z = pl.program_id(0), place[2]
    heads, experts = table.shape[1], table.shape[2]

    @pl.when(b == 0)
    def _():
        src, dst = iota((512, 512), 0), iota((512, 512), 1)
        order = one_hot(dst == ((src & 255) >> 5) * 64 + 2 * (src & 31) + (src >> 8))

        def one_head(h, carry):
            for e in range(experts):
                t = table[:, h, e].reshape(256, LANES).T
                first = pl.multiple_of(h * experts * HALF, experts * HALF) + e * HALF
                flipped[pl.ds(first, HALF), :] = jnp.concatenate([t[:HALF], t[HALF:]], axis=1)
            whole = pl.ds(pl.multiple_of(h * experts * HALF, experts * HALF), experts * HALF)
            ordered[whole, :] = dot(flipped[whole, :], order).astype(bf16)
            return carry

        lax.fori_loop(0, heads, one_head, 0)

    for k in range(heads * TOP):
        e = ids[(z * PLANE + b) * heads * TOP + k]
        first = pl.multiple_of(((k // TOP) * experts + e) * HALF, HALF)
        out[0, k * HALF : (k + 1) * HALF, :] = ordered[pl.ds(first, HALF), :]


def mix_kernel(place, attended, gates_in, rows, near, far, lhs, natural, spread):
    q, core = pl.program_id(0), place[1] & 1
    heads = rows.shape[1] // LANES
    left = iota((BLK, LANES), 1) < HALF

    @pl.when(q == 0)
    def _():
        spread[...] = one_hot(iota(spread.shape, 0) == (iota(spread.shape, 1) >> 6))

    for bb in range(2):
        gates = dot(gates_in[bb], spread[...])
        for h in range(heads):
            packed = attended[h, q].astype(f32)
            both = jnp.where(left == (bb == 0), packed, pltpu.roll(packed, HALF, 1))
            cols = slice(h * LANES, (h + 1) * LANES)
            lhs[bb, :, cols] = (both * gates[:, cols]).astype(bf16)
    for bb in range(2):
        flat = dot(lhs[bb], rows[bb]).astype(bf16)
        for g in range(4):
            natural[g, bb] = flat[:, g * LANES : (g + 1) * LANES]
    for y in range(2):
        near[y] = natural[2 * y + core]
        far[y] = natural[2 * y + (1 - core)]


def place_kernel(pieces, out):
    width = out.shape[1] // 2
    summed = [(pieces[i].astype(f32) + pieces[PLANE + i].astype(f32)).astype(bf16) for i in range(PLANE)]
    for low in range(2):
        own = slice(low * HALF, (low + 1) * HALF)
        for m in range(PLANE // 2):
            out[:, low * width + m * LANES : low * width + (m + 1) * LANES] = jnp.concatenate(
                [summed[2 * m][:, own], summed[2 * m + 1][:, own]], axis=1
            )


def swap(x, axis):
    return lax.ppermute(x, axis, [(0, 1), (1, 0)])


def plane_exchange(x):
    return lax.all_to_all(x, PLANE_AXES, split_axis=0, concat_axis=0, tiled=True)


def ring_step(x, way):
    return lax.ppermute(x, "z", [(i, (i + way) % SLABS) for i in range(SLABS)])


def add(a, b):
    return (a.astype(f32) + b.astype(f32)).astype(bf16)


def body(features, queries, keys, router, value_experts, output_experts, expert_ids):
    z = lax.axis_index("z")
    group = lax.axis_index(HEAD_AXES)
    seq = lax.axis_index(SEQ_AXES)
    place = jnp.stack([seq, group, z]).astype(i32)
    ids = expert_ids.reshape(-1)
    heads = value_experts.shape[0]
    scale = 1.0 / math.sqrt(HALF)

    value_table = lax.all_gather(value_experts, "z", axis=0, tiled=False)
    pairs = pl.pallas_call(
        lambda *refs: pair_kernel(scale, *refs),
        out_shape=jax.ShapeDtypeStruct((PLANE, BLK, LANES), bf16),
        in_specs=[vmem, vmem],
        out_specs=vmem,
        cost_estimate=cost(0, 500_000),
    )(queries, keys)
    pairs = plane_exchange(pairs)

    own_keys = pl.pallas_call(
        key_kernel,
        out_shape=jax.ShapeDtypeStruct((LANES, PLANE // 2 * BLK), bf16),
        in_specs=[vmem],
        out_specs=vmem,
        cost_estimate=cost(0, 400_000),
    )(pairs)
    keys = [own_keys] * SLABS
    keys[1], keys[7] = ring_step(own_keys, 1), ring_step(own_keys, -1)
    over_y = swap(features, "yh")
    over_c = swap(features, "c")
    over_yc = swap(over_y, "c")
    keys[2], keys[6] = ring_step(keys[1], 1), ring_step(keys[7], -1)
    message = pl.pallas_call(
        message_kernel,
        out_shape=jax.ShapeDtypeStruct((PLANE, BLK, 5 * LANES), bf16),
        in_specs=[smem, smem] + [vmem] * 5,
        out_specs=vmem,
        compiler_params=small,
        cost_estimate=cost(2 * BLK * LANES * 4096 * 2, 3_000_000),
    )(ids, place, features, over_c, over_y, over_yc, router)
    keys[3], keys[5] = ring_step(keys[2], 1), ring_step(keys[6], -1)
    message = plane_exchange(message)

    keys[4] = ring_step(keys[3], 1)
    message, keys = lax.optimization_barrier((message, keys))

    slab = PLANE * BLK
    partial = pl.pallas_call(
        value_kernel,
        out_shape=jax.ShapeDtypeStruct((PLANE, PLANE // 2, BLK, LANES), bf16),
        in_specs=[smem, smem, vmem, vmem],
        out_specs=vmem,
        compiler_params=small,
        cost_estimate=cost(2 * 48 * 256 * 256 * 256, 6_000_000),
    )(ids, place, message, value_table)
    _, pairs = lax.optimization_barrier((partial, pairs))
    probs, sums = pl.pallas_call(
        weight_kernel,
        grid=(PLANE + 1,),
        out_shape=(
            jax.ShapeDtypeStruct((SLABS, 2, slab, slab // 2), bf16),
            jax.ShapeDtypeStruct((slab, LANES), f32),
        ),
        in_specs=[smem, pl.BlockSpec((1, BLK, LANES), lambda i: (jnp.minimum(i, PLANE - 1), 0, 0))] + [vmem] * SLABS,
        out_specs=(
            pl.BlockSpec((SLABS, 2, BLK, slab // 2), lambda i: (0, 0, jnp.maximum(i - 1, 0), 0)),
            pl.BlockSpec((BLK, LANES), lambda i: (jnp.maximum(i - 1, 0), 0)),
        ),
        scratch_shapes=[
            pltpu.VMEM((SLABS, 2 * BLK, slab // 2), f32),
            pltpu.VMEM((SLABS, 2 * BLK, slab // 2), f32),
            pltpu.VMEM((BLK, LANES), f32),
            pltpu.VMEM((BLK, LANES), f32),
            pltpu.VMEM((BLK, LANES), f32),
        ],
        compiler_params=large,
        cost_estimate=cost(2 * slab * SLABS * slab * 128, 18_000_000, slab * slab * SLABS),
    )(place, pairs, *keys)

    partial = plane_exchange(partial)
    own_values = jnp.sum(partial.astype(f32), axis=0).astype(bf16).reshape(slab // 2, LANES)
    own_values, sums = lax.optimization_barrier((own_values, sums))
    values = [own_values] * SLABS
    output_table = lax.all_gather(output_experts, "z", axis=0, tiled=False)

    def weighted(near, carried, last):
        steps = len(near)
        full = pl.BlockSpec((slab, LANES), lambda i, at: (0, 0))
        one = pl.BlockSpec((slab // 2, LANES), lambda i, at: (0, 0))

        def pick(i, at):
            s = jnp.int32(near[-1])
            for k in range(steps - 1):
                s = jnp.where(i == k, near[k], s)
            return (jnp.where(s <= at[2], s, 0), 0, 0, 0)

        if last:
            out_shape = jax.ShapeDtypeStruct((PLANE, PLANE // 2, BLK, LANES), bf16)
            out_spec = pl.BlockSpec(out_shape.shape, lambda i, at: (0, 0, 0, 0))
        else:
            out_shape = jax.ShapeDtypeStruct((slab, LANES), f32)
            out_spec = full
        return pl.pallas_call(
            lambda *refs: attend_kernel(near, len(carried), last, *refs),
            grid_spec=pltpu.PrefetchScalarGridSpec(
                num_scalar_prefetch=1,
                grid=(steps,),
                in_specs=[pl.BlockSpec((1, 2, slab, slab // 2), pick)]
                + [one] * steps
                + [full] * len(carried),
                out_specs=out_spec,
                scratch_shapes=[pltpu.VMEM((slab, LANES), f32)],
            ),
            out_shape=out_shape,
            compiler_params=large,
            cost_estimate=cost(steps * 2 * slab * slab * 128, steps * 2_000_000),
        )(place, probs, *[values[s] for s in near], *carried)

    values[1], values[7] = ring_step(own_values, 1), ring_step(own_values, -1)
    acc = weighted((0,), (), False)
    values[1], values[7], acc = lax.optimization_barrier((values[1], values[7], acc))
    values[2], values[6] = ring_step(values[1], 1), ring_step(values[7], -1)
    acc = weighted((1, 7), (acc,), False)
    values[2], values[6], acc = lax.optimization_barrier((values[2], values[6], acc))
    values[3], values[5] = ring_step(values[2], 1), ring_step(values[6], -1)
    acc = weighted((2, 6), (acc,), False)
    values[3], values[5], acc = lax.optimization_barrier((values[3], values[5], acc))
    values[4] = ring_step(values[3], 1)
    acc = weighted((3, 5), (acc,), False)
    attended = weighted((4,), (acc, sums), True)
    _, output_table = lax.optimization_barrier((attended, output_table))
    attended = plane_exchange(attended)

    width = heads * TOP * HALF
    rows = pl.pallas_call(
        chosen_kernel,
        grid=(PLANE,),
        out_shape=jax.ShapeDtypeStruct((PLANE, width, 512), bf16),
        in_specs=[smem, smem, vmem],
        out_specs=pl.BlockSpec((1, width, 512), lambda b: (b, 0, 0)),
        scratch_shapes=[pltpu.VMEM((heads * 8 * HALF, 512), bf16)] * 2,
        compiler_params=large,
        cost_estimate=cost(0, 20_000_000),
    )(ids, place, output_table)
    half_out = jax.ShapeDtypeStruct((2, PLANE, BLK, LANES), bf16)
    half_spec = pl.BlockSpec((2, 2, BLK, LANES), lambda b: (0, b, 0, 0))
    near, far = pl.pallas_call(
        mix_kernel,
        grid=(PLANE // 2,),
        out_shape=(half_out, half_out),
        in_specs=[
            smem,
            vmem,
            pl.BlockSpec((2, BLK, LANES), lambda b: (b, 0, 4)),
            pl.BlockSpec((2, width, 512), lambda b: (b, 0, 0)),
        ],
        out_specs=(half_spec, half_spec),
        scratch_shapes=[
            pltpu.VMEM((2, BLK, width), bf16),
            pltpu.VMEM((4, 2, BLK, LANES), bf16),
            pltpu.VMEM((LANES, width), bf16),
        ],
        compiler_params=small,
        cost_estimate=cost(2 * 8 * 128 * 768 * 512, 8_000_000),
    )(place, attended, message, rows)
    near = add(near, swap(far, "c"))
    mixed = lax.all_to_all(
        near.reshape(2 * PLANE, BLK, LANES), ("yh",) + PLANE_AXES, split_axis=0, concat_axis=0, tiled=True
    )
    return pl.pallas_call(
        place_kernel,
        out_shape=jax.ShapeDtypeStruct(features.shape, bf16),
        in_specs=[vmem],
        out_specs=vmem,
        cost_estimate=cost(0, 600_000),
    )(mixed)


def solution(mesh):
    fine = Mesh(mesh.devices.reshape(SLABS, 2, 4, 2, 2), AXES)
    return jax.shard_map(
        body,
        mesh=fine,
        in_specs=(
            P(SEQ_AXES, HEAD_AXES),
            P(SEQ_AXES, HEAD_AXES),
            P(SEQ_AXES, HEAD_AXES),
            P(HEAD_AXES, None),
            P(HEAD_AXES, None, SEQ_AXES, None),
            P(HEAD_AXES, None, SEQ_AXES, None),
            P(None, HEAD_AXES, None),
        ),
        out_specs=P(SEQ_AXES, HEAD_AXES),
        check_vma=False,
    )
```

```python
import math

import jax
import jax.numpy as jnp
from jax import lax
from jax.experimental import pallas as pl
from jax.experimental.pallas import tpu as pltpu
from jax.sharding import Mesh, PartitionSpec as P

TOP = 2
BLK = 128
SLABS = 8
PLANE = 8
HALF = 64
LANES = 128
AXES = ("z", "yl", "x", "yh", "c")
SEQ_AXES = ("z", "yl", "x")
HEAD_AXES = ("yh", "c")
PLANE_AXES = ("yl", "x")
bf16 = jnp.bfloat16
f32 = jnp.float32
i32 = jnp.int32
masked_score = -1e30
MIB = 1024 * 1024

smem = pl.BlockSpec(memory_space=pltpu.SMEM)
vmem = pl.BlockSpec(memory_space=pltpu.VMEM)
large = pltpu.CompilerParams(vmem_limit_bytes=56 * MIB)
small = pltpu.CompilerParams(vmem_limit_bytes=20 * MIB)


def cost(flops, nbytes, trans=0):
    return pl.CostEstimate(flops=flops, bytes_accessed=nbytes, transcendentals=trans)


def iota(shape, dim):
    return lax.broadcasted_iota(i32, shape, dim)


def one_hot(mask):
    return jnp.where(mask, 1.0, 0.0).astype(bf16)


def nt_dot(a, b):
    return lax.dot_general(a, b, (((1,), (1,)), ((), ())), preferred_element_type=f32)


def dot(a, b):
    return jnp.dot(a, b, preferred_element_type=f32)


def message_kernel(ids, place, f0, f1, f2, f3, router, out):
    slots = router.shape[0] // 8 * TOP
    quarter = f0.shape[1]
    seq, group = place[0], place[1]
    row, col = iota((LANES, router.shape[0]), 0), iota((LANES, router.shape[0]), 1)
    target = jnp.full(row.shape, -1, i32)
    for k in range(slots):
        target = jnp.where(row == k, (k // TOP) * 8 + ids[seq * slots + k], target)
    chosen = one_hot(col == target)
    logits = jnp.zeros((BLK, LANES), f32)
    for rel, part in enumerate((f0, f1, f2, f3)):
        first = pl.multiple_of((group ^ rel) * quarter, quarter)
        rows = dot(chosen, router[:, pl.ds(first, quarter)]).astype(bf16)
        logits = logits + nt_dot(part[...], rows)
        for pi in range(PLANE):
            low = part[:, pi * HALF : (pi + 1) * HALF]
            high = part[:, quarter // 2 + pi * HALF : quarter // 2 + (pi + 1) * HALF]
            out[pi, :, rel * LANES : (rel + 1) * LANES] = jnp.concatenate([low, high], axis=1)
    gates = jax.nn.sigmoid(logits).astype(bf16)
    for pi in range(PLANE):
        out[pi, :, 4 * LANES :] = gates


def pair_kernel(scale, queries, keys, out):
    for i in range(PLANE):
        if i * HALF < queries.shape[1]:
            own = slice(i * HALF, (i + 1) * HALF)
            out[i] = jnp.concatenate([queries[:, own] * bf16(scale), keys[:, own]], axis=1)
        else:
            out[i] = jnp.zeros((BLK, LANES), bf16)


def key_kernel(pairs, out):
    for q in range(PLANE // 2):
        both = jnp.concatenate([pairs[2 * q][:, HALF:], pairs[2 * q + 1][:, HALF:]], axis=1)
        out[:, q * BLK : (q + 1) * BLK] = both.T


def value_kernel(ids, place, message, table, out):
    heads = table.shape[1]
    z, group = place[2], place[1]
    src, dst = iota((512, 512), 0), iota((512, 512), 1)
    within = src & 63
    source_z = ((src >> 7) ^ group) * 2 + ((src >> 6) & 1)
    split = one_hot(dst == (within & 1) * 256 + source_z * 32 + (within >> 1))
    left = iota((BLK, LANES), 1) < HALF

    def two_blocks(q, carry):
        done = []
        for bb in range(2):
            b = 2 * q + bb
            x = dot(message[b, :, 0:512], split).astype(bf16)
            x = jnp.concatenate([x[:, :256], x[:, 256:]], axis=0)
            gates = message[b, :, 512:].astype(f32)
            sums = []
            for h in range(heads):
                total = 0.0
                picked = [
                    table[:, h, ids[((z * PLANE + b) * heads + h) * TOP + j]].reshape(256, LANES)
                    for j in range(TOP)
                ]
                r = dot(x, jnp.concatenate(picked, axis=1))
                for j in range(TOP):
                    cols = slice(j * LANES, (j + 1) * LANES)
                    k = h * TOP + j
                    total = total + gates[:, k : k + 1] * jnp.where(left, r[:BLK, cols], r[BLK:, cols])
                sums.append(total)
            done.append(sums)
        for h in range(heads):
            first, second = done[0][h], done[1][h]
            crossed = pltpu.roll(jnp.where(left, second, first), HALF, 1)
            out[h, q] = (jnp.where(left, first, second) + crossed).astype(bf16)
        for h in range(heads, PLANE):
            out[h, q] = jnp.zeros((BLK, LANES), bf16)
        return carry

    lax.fori_loop(0, PLANE // 2, two_blocks, 0)


def weight_kernel(place, pairs, k0, k1, k2, k3, k4, k5, k6, k7, probs, sums, even, odd, even_top, odd_top, totals):
    step, z = pl.program_id(0), place[2]
    block = jnp.minimum(step, PLANE - 1)
    zero = jnp.zeros((BLK, HALF), bf16)
    own = pairs[0][:, :HALF]
    q = jnp.concatenate(
        [jnp.concatenate([own, zero], axis=1), jnp.concatenate([zero, own], axis=1)], axis=0
    )

    def run(scores, tops, old_scores, old_tops):
        top = jnp.broadcast_to(jnp.max(old_tops[...], axis=1, keepdims=True), (BLK, LANES))
        tops[...] = jnp.full((BLK, LANES), masked_score, f32)
        totals[...] = jnp.zeros(totals.shape, f32)
        every = (k0, k1, k2, k3, k4, k5, k6, k7)
        for first in range(0, SLABS, 2):

            @pl.when(first <= z)
            def _():
                best, total = tops[...], totals[...]
                for s in (first, first + 1):
                    for c in range(2):
                        wide = slice(c * 256, (c + 1) * 256)
                        got = dot(q, every[s][:, wide])
                        if s == 0:
                            row, col = iota(got.shape, 0), iota(got.shape, 1) + c * 256
                            key_pos = (2 * (col >> 7) + (row >> 7)) * BLK + (col & 127)
                            got = jnp.where(key_pos <= block * BLK + (row & 127), got, masked_score)
                        if s % 2 == 1:
                            got = jnp.where(s <= z, got, masked_score)
                        scores[s, :, wide] = got
                        for rows in (slice(0, BLK), slice(BLK, 2 * BLK)):
                            for cols in (slice(0, LANES), slice(LANES, 2 * LANES)):
                                best = jnp.maximum(best, got[rows, cols])
                        for bb in range(2):
                            for part in range(2 * c, 2 * c + 2):
                                cols = slice(part * LANES, (part + 1) * LANES)
                                p = jnp.exp(old_scores[s, bb * BLK : (bb + 1) * BLK, cols] - top)
                                total = total + p
                                probs[s, bb, :, cols] = p.astype(bf16)
                tops[...], totals[...] = best, total

        sums[...] = jnp.broadcast_to(jnp.sum(totals[...], axis=1, keepdims=True), (BLK, LANES))

    @pl.when(step % 2 == 0)
    def _():
        run(even, even_top, odd, odd_top)

    @pl.when(step % 2 == 1)
    def _():
        run(odd, odd_top, even, even_top)


def attend_kernel(near, carried, last, place, probs, *refs):
    values, refs = refs[: len(near)], refs[len(near) :]
    acc_in, out, acc = refs[:carried], refs[carried], refs[carried + 1]
    step, z = pl.program_id(0), place[2]
    left = iota((PLANE * BLK, LANES), 1) < HALF

    @pl.when(step == 0)
    def _():
        acc[...] = acc_in[0][...] if carried else jnp.zeros(acc.shape, f32)

    for k, s in enumerate(near):

        @pl.when((step == k) & (s <= z))
        def _():
            got = [dot(probs[0, bb], values[k][...]) for bb in range(2)]
            acc[...] += jnp.where(left, got[0], got[1])

    @pl.when(step == len(near) - 1)
    def _():
        if not last:
            out[...] = acc[...]
        else:
            left = iota((BLK, LANES), 1) < HALF
            for q in range(PLANE // 2):
                pair = []
                for bb in range(2):
                    rows = slice((2 * q + bb) * BLK, (2 * q + bb + 1) * BLK)
                    o = acc[rows]
                    pair.append((o + pltpu.roll(o, HALF, 1)) / acc_in[1][rows])
                packed = jnp.where(left, pair[0], pair[1]).astype(bf16)
                for pi in range(PLANE):
                    out[pi, q] = packed


def chosen_kernel(ids, place, table, out, flipped, ordered):
    b, z = pl.program_id(0), place[2]
    heads, experts = table.shape[1], table.shape[2]

    @pl.when(b == 0)
    def _():
        src, dst = iota((512, 512), 0), iota((512, 512), 1)
        order = one_hot(dst == ((src & 255) >> 5) * 64 + 2 * (src & 31) + (src >> 8))

        def one_head(h, carry):
            for e in range(experts):
                t = table[:, h, e].reshape(256, LANES).T
                first = pl.multiple_of(h * experts * HALF, experts * HALF) + e * HALF
                flipped[pl.ds(first, HALF), :] = jnp.concatenate([t[:HALF], t[HALF:]], axis=1)
            whole = pl.ds(pl.multiple_of(h * experts * HALF, experts * HALF), experts * HALF)
            ordered[whole, :] = dot(flipped[whole, :], order).astype(bf16)
            return carry

        lax.fori_loop(0, heads, one_head, 0)

    for k in range(heads * TOP):
        e = ids[(z * PLANE + b) * heads * TOP + k]
        first = pl.multiple_of(((k // TOP) * experts + e) * HALF, HALF)
        out[0, k * HALF : (k + 1) * HALF, :] = ordered[pl.ds(first, HALF), :]


def mix_kernel(place, attended, gates_in, rows, near, far, lhs, natural, spread):
    q, core = pl.program_id(0), place[1] & 1
    heads = rows.shape[1] // LANES
    left = iota((BLK, LANES), 1) < HALF

    @pl.when(q == 0)
    def _():
        spread[...] = one_hot(iota(spread.shape, 0) == (iota(spread.shape, 1) >> 6))

    for bb in range(2):
        gates = dot(gates_in[bb], spread[...])
        for h in range(heads):
            packed = attended[h, q].astype(f32)
            both = jnp.where(left == (bb == 0), packed, pltpu.roll(packed, HALF, 1))
            cols = slice(h * LANES, (h + 1) * LANES)
            lhs[bb, :, cols] = (both * gates[:, cols]).astype(bf16)
    for bb in range(2):
        flat = dot(lhs[bb], rows[bb]).astype(bf16)
        for g in range(4):
            natural[g, bb] = flat[:, g * LANES : (g + 1) * LANES]
    for y in range(2):
        near[y] = natural[2 * y + core]
        far[y] = natural[2 * y + (1 - core)]


def place_kernel(pieces, out):
    width = out.shape[1] // 2
    summed = [(pieces[i].astype(f32) + pieces[PLANE + i].astype(f32)).astype(bf16) for i in range(PLANE)]
    for low in range(2):
        own = slice(low * HALF, (low + 1) * HALF)
        for m in range(PLANE // 2):
            out[:, low * width + m * LANES : low * width + (m + 1) * LANES] = jnp.concatenate(
                [summed[2 * m][:, own], summed[2 * m + 1][:, own]], axis=1
            )


def swap(x, axis):
    return lax.ppermute(x, axis, [(0, 1), (1, 0)])


def plane_exchange(x):
    return lax.all_to_all(x, PLANE_AXES, split_axis=0, concat_axis=0, tiled=True)


def ring_step(x, way):
    return lax.ppermute(x, "z", [(i, (i + way) % SLABS) for i in range(SLABS)])


def add(a, b):
    return (a.astype(f32) + b.astype(f32)).astype(bf16)


def body(features, queries, keys, router, value_experts, output_experts, expert_ids):
    z = lax.axis_index("z")
    group = lax.axis_index(HEAD_AXES)
    seq = lax.axis_index(SEQ_AXES)
    place = jnp.stack([seq, group, z]).astype(i32)
    ids = expert_ids.reshape(-1)
    heads = value_experts.shape[0]
    scale = 1.0 / math.sqrt(HALF)

    value_table = lax.all_gather(value_experts, "z", axis=0, tiled=False)
    pairs = pl.pallas_call(
        lambda *refs: pair_kernel(scale, *refs),
        out_shape=jax.ShapeDtypeStruct((PLANE, BLK, LANES), bf16),
        in_specs=[vmem, vmem],
        out_specs=vmem,
        cost_estimate=cost(0, 500_000),
    )(queries, keys)
    pairs = plane_exchange(pairs)

    own_keys = pl.pallas_call(
        key_kernel,
        out_shape=jax.ShapeDtypeStruct((LANES, PLANE // 2 * BLK), bf16),
        in_specs=[vmem],
        out_specs=vmem,
        cost_estimate=cost(0, 400_000),
    )(pairs)
    keys = [own_keys] * SLABS
    keys[1], keys[7] = ring_step(own_keys, 1), ring_step(own_keys, -1)
    over_y = swap(features, "yh")
    over_c = swap(features, "c")
    over_yc = swap(over_y, "c")
    keys[2], keys[6] = ring_step(keys[1], 1), ring_step(keys[7], -1)
    message = pl.pallas_call(
        message_kernel,
        out_shape=jax.ShapeDtypeStruct((PLANE, BLK, 5 * LANES), bf16),
        in_specs=[smem, smem] + [vmem] * 5,
        out_specs=vmem,
        compiler_params=small,
        cost_estimate=cost(2 * BLK * LANES * 4096 * 2, 3_000_000),
    )(ids, place, features, over_c, over_y, over_yc, router)
    keys[3], keys[5] = ring_step(keys[2], 1), ring_step(keys[6], -1)
    message = plane_exchange(message)

    keys[4] = ring_step(keys[3], 1)
    message, keys = lax.optimization_barrier((message, keys))

    slab = PLANE * BLK
    partial = pl.pallas_call(
        value_kernel,
        out_shape=jax.ShapeDtypeStruct((PLANE, PLANE // 2, BLK, LANES), bf16),
        in_specs=[smem, smem, vmem, vmem],
        out_specs=vmem,
        compiler_params=small,
        cost_estimate=cost(2 * 48 * 256 * 256 * 256, 6_000_000),
    )(ids, place, message, value_table)
    _, pairs = lax.optimization_barrier((partial, pairs))
    probs, sums = pl.pallas_call(
        weight_kernel,
        grid=(PLANE + 1,),
        out_shape=(
            jax.ShapeDtypeStruct((SLABS, 2, slab, slab // 2), bf16),
            jax.ShapeDtypeStruct((slab, LANES), f32),
        ),
        in_specs=[smem, pl.BlockSpec((1, BLK, LANES), lambda i: (jnp.minimum(i, PLANE - 1), 0, 0))] + [vmem] * SLABS,
        out_specs=(
            pl.BlockSpec((SLABS, 2, BLK, slab // 2), lambda i: (0, 0, jnp.maximum(i - 1, 0), 0)),
            pl.BlockSpec((BLK, LANES), lambda i: (jnp.maximum(i - 1, 0), 0)),
        ),
        scratch_shapes=[
            pltpu.VMEM((SLABS, 2 * BLK, slab // 2), f32),
            pltpu.VMEM((SLABS, 2 * BLK, slab // 2), f32),
            pltpu.VMEM((BLK, LANES), f32),
            pltpu.VMEM((BLK, LANES), f32),
            pltpu.VMEM((BLK, LANES), f32),
        ],
        compiler_params=large,
        cost_estimate=cost(2 * slab * SLABS * slab * 128, 18_000_000, slab * slab * SLABS),
    )(place, pairs, *keys)

    partial = plane_exchange(partial)
    own_values = jnp.sum(partial.astype(f32), axis=0).astype(bf16).reshape(slab // 2, LANES)
    own_values, sums = lax.optimization_barrier((own_values, sums))
    values = [own_values] * SLABS
    output_table = lax.all_gather(output_experts, "z", axis=0, tiled=False)

    def weighted(near, carried, last):
        steps = len(near)
        full = pl.BlockSpec((slab, LANES), lambda i, at: (0, 0))
        one = pl.BlockSpec((slab // 2, LANES), lambda i, at: (0, 0))

        def pick(i, at):
            s = jnp.int32(near[-1])
            for k in range(steps - 1):
                s = jnp.where(i == k, near[k], s)
            return (jnp.where(s <= at[2], s, 0), 0, 0, 0)

        if last:
            out_shape = jax.ShapeDtypeStruct((PLANE, PLANE // 2, BLK, LANES), bf16)
            out_spec = pl.BlockSpec(out_shape.shape, lambda i, at: (0, 0, 0, 0))
        else:
            out_shape = jax.ShapeDtypeStruct((slab, LANES), f32)
            out_spec = full
        return pl.pallas_call(
            lambda *refs: attend_kernel(near, len(carried), last, *refs),
            grid_spec=pltpu.PrefetchScalarGridSpec(
                num_scalar_prefetch=1,
                grid=(steps,),
                in_specs=[pl.BlockSpec((1, 2, slab, slab // 2), pick)]
                + [one] * steps
                + [full] * len(carried),
                out_specs=out_spec,
                scratch_shapes=[pltpu.VMEM((slab, LANES), f32)],
            ),
            out_shape=out_shape,
            compiler_params=small,
            cost_estimate=cost(steps * 2 * slab * slab * 128, steps * 2_000_000),
        )(place, probs, *[values[s] for s in near], *carried)

    values[1], values[7] = ring_step(own_values, 1), ring_step(own_values, -1)
    values[2], values[6] = ring_step(values[1], 1), ring_step(values[7], -1)
    acc = weighted((0, 1, 7), (), False)
    values[2], values[6], acc = lax.optimization_barrier((values[2], values[6], acc))
    values[3], values[5] = ring_step(values[2], 1), ring_step(values[6], -1)
    acc = weighted((2, 6), (acc,), False)
    values[3], values[5], acc = lax.optimization_barrier((values[3], values[5], acc))
    values[4] = ring_step(values[3], 1)
    acc = weighted((3, 5), (acc,), False)
    attended = weighted((4,), (acc, sums), True)
    _, output_table = lax.optimization_barrier((attended, output_table))
    attended = plane_exchange(attended)

    width = heads * TOP * HALF
    rows = pl.pallas_call(
        chosen_kernel,
        grid=(PLANE,),
        out_shape=jax.ShapeDtypeStruct((PLANE, width, 512), bf16),
        in_specs=[smem, smem, vmem],
        out_specs=pl.BlockSpec((1, width, 512), lambda b: (b, 0, 0)),
        scratch_shapes=[pltpu.VMEM((heads * 8 * HALF, 512), bf16)] * 2,
        compiler_params=large,
        cost_estimate=cost(0, 20_000_000),
    )(ids, place, output_table)
    half_out = jax.ShapeDtypeStruct((2, PLANE, BLK, LANES), bf16)
    half_spec = pl.BlockSpec((2, 2, BLK, LANES), lambda b: (0, b, 0, 0))
    near, far = pl.pallas_call(
        mix_kernel,
        grid=(PLANE // 2,),
        out_shape=(half_out, half_out),
        in_specs=[
            smem,
            vmem,
            pl.BlockSpec((2, BLK, LANES), lambda b: (b, 0, 4)),
            pl.BlockSpec((2, width, 512), lambda b: (b, 0, 0)),
        ],
        out_specs=(half_spec, half_spec),
        scratch_shapes=[
            pltpu.VMEM((2, BLK, width), bf16),
            pltpu.VMEM((4, 2, BLK, LANES), bf16),
            pltpu.VMEM((LANES, width), bf16),
        ],
        compiler_params=small,
        cost_estimate=cost(2 * 8 * 128 * 768 * 512, 8_000_000),
    )(place, attended, message, rows)
    near = add(near, swap(far, "c"))
    mixed = lax.all_to_all(
        near.reshape(2 * PLANE, BLK, LANES), ("yh",) + PLANE_AXES, split_axis=0, concat_axis=0, tiled=True
    )
    return pl.pallas_call(
        place_kernel,
        out_shape=jax.ShapeDtypeStruct(features.shape, bf16),
        in_specs=[vmem],
        out_specs=vmem,
        cost_estimate=cost(0, 600_000),
    )(mixed)


def solution(mesh):
    fine = Mesh(mesh.devices.reshape(SLABS, 2, 4, 2, 2), AXES)
    return jax.shard_map(
        body,
        mesh=fine,
        in_specs=(
            P(SEQ_AXES, HEAD_AXES),
            P(SEQ_AXES, HEAD_AXES),
            P(SEQ_AXES, HEAD_AXES),
            P(HEAD_AXES, None),
            P(HEAD_AXES, None, SEQ_AXES, None),
            P(HEAD_AXES, None, SEQ_AXES, None),
            P(None, HEAD_AXES, None),
        ),
        out_specs=P(SEQ_AXES, HEAD_AXES),
        check_vma=False,
    )
```
